32 devices in a mesh: gx: 4 (over z), gy: 4 (over x, core), gz: 2 (over y).
Axes of the slice: x: 2, y: 2, z: 4, core: 2. Of those that a mesh axis runs over, the one named last changes fastest.
Arguments:
- orbitals: float32 [4, 4, 2, 96, 4096], P('gx', 'gy', 'gz'), may hold values from -6 to 6
- potential: float32 [32, 32, 16], P('gx', 'gy', 'gz'), may hold values from -1.5 to 1.5
- coefficients: float32 [4, 4, 2, 96, 256], P('gx', 'gy', 'gz'), may hold values from -0.6 to 0.6
Outputs:
- filtered_coefficients: float32 [4, 4, 2, 96, 256], P('gx', 'gy', 'gz')
The draws below stay inside these ranges and needn't reach their ends.
All inputs are finite; a program needn't handle non-finite values.
Results may differ from the reference program's by a relative error of at most 0.0003.
Values sent between devices are 32-bit elements; how exact they have to be, the bound alone decides.
A program may use at most 64 MiB of HBM per device.

```python
import jax
import jax.numpy as jnp
from jax import lax

ORBITAL_TOTAL = 96
COEFFICIENT_COLS = 256
EDGE = 8
CHEB = 2
NEWTON = 6
DG_STEPS = 3
ELEMENTS_FIRST = 4
ELEMENTS_SECOND = 4
ELEMENTS_THIRD = 2
NXC = 32
NYC = 32
NZC = 16
EXTENDED_CELLS = 4096


def levels(stream_key, extent, shards, low, largest):
    gain, own = 1.0, jax.random.fold_in(stream_key, 6)
    for axis_at, parts in shards:
        heights = jnp.exp(jax.random.uniform(jax.random.fold_in(own, axis_at), (parts,), jnp.float32, low / len(shards), largest / len(shards)))
        gain = gain * jnp.repeat(heights, extent[axis_at] // parts).reshape([-1 if axis == axis_at else 1 for axis in range(len(extent))])
    return gain


def noise(rng, shape, width, reach, pieces=(), held_as=jnp.bfloat16):
    drawn = width * jax.random.normal(rng, shape, jnp.float32)
    if pieces:
        drawn = drawn * levels(rng, shape, pieces, -0.22, 0.18)
    return jnp.clip(drawn, -reach, reach).astype(held_as)


def setup_inputs(seed: int = 0) -> dict:
    splits = jax.random.split(jax.random.key(seed), 4)
    orbitals = noise(splits[0], (ELEMENTS_FIRST, ELEMENTS_SECOND, ELEMENTS_THIRD, ORBITAL_TOTAL, EXTENDED_CELLS), 1.0, 6.0, ((0, 4), (1, 4), (2, 2)), jnp.float32)
    potential = jnp.clip(jax.random.uniform(splits[1], (NXC, NYC, NZC), jnp.float32, -1.5, 1.5) * levels(splits[1], (NXC, NYC, NZC), ((0, 4), (1, 4), (2, 2)), -0.4, 0.0), -1.5, 1.5)
    coefficients = noise(splits[2], (ELEMENTS_FIRST, ELEMENTS_SECOND, ELEMENTS_THIRD, ORBITAL_TOTAL, COEFFICIENT_COLS), 0.1, 0.6, ((0, 4), (1, 4), (2, 2)), jnp.float32)
    return dict(orbitals=orbitals, potential=potential, coefficients=coefficients)


cutoff = 1.0

def matmul(left, right):
    return jnp.dot(left, right, precision=lax.Precision.HIGHEST, preferred_element_type=jnp.float32)

def box_masks(length):
    position = jnp.arange(length ** 3, dtype=jnp.int32)
    coordinates = (position // (length * length), position // length % length, position % length)
    mask_list = []
    for coordinate, stride in zip(coordinates, (length * length, length, 1)):
        mask_list.append((stride, (coordinate > 0).astype(jnp.float32), (coordinate < length - 1).astype(jnp.float32)))
    return mask_list

def apply_box(vectors, potential_flat, length):
    area = length * length
    cells = length ** 3
    padded = jnp.pad(vectors, ((0, 0), (area, area)))
    total = jnp.zeros_like(vectors)
    for stride, lower_ok, upper_ok in box_masks(length):
        total = total + lower_ok * padded[:, area - stride:area - stride + cells] + upper_ok * padded[:, area + stride:area + stride + cells]
    return (3.0 + potential_flat) * vectors - 0.5 * total

def chebyshev(operator, initial, degree, centre, half_width):
    prior_vectors = initial
    current = (operator(initial) - centre * initial) / half_width
    for repeat in range(degree - 1):
        following = 2.0 * (operator(current) - centre * current) / half_width - prior_vectors
        prior_vectors, current = (current, following)
    return current

def inverse_root(intersection, newton_count):
    sigma = jnp.sqrt(jnp.sum(intersection * intersection))
    identity = jnp.eye(intersection.shape[0], dtype=jnp.float32)
    current = intersection / sigma
    inverse = identity
    for repeat in range(newton_count):
        factor = 1.5 * identity - 0.5 * matmul(inverse, current)
        current = matmul(current, factor)
        inverse = matmul(factor, inverse)
    return inverse / jnp.sqrt(sigma)

def element_basis(orbital_rows, ext_potential, length, centre, half_width):
    doubled = 2 * length
    potential_flat = ext_potential.reshape(doubled ** 3)

    def extended_operator(vectors):
        return apply_box(vectors, potential_flat, doubled)
    filtered = chebyshev(extended_operator, orbital_rows, CHEB, centre, half_width)
    lower = length // 2
    restricted = filtered.reshape(-1, doubled, doubled, doubled)[:, lower:lower + length, lower:lower + length, lower:lower + length]
    restricted = restricted.reshape(-1, length ** 3)
    intersection = matmul(restricted, restricted.T)
    basis = matmul(inverse_root(intersection, NEWTON), restricted)
    own_potential = ext_potential[lower:lower + length, lower:lower + length, lower:lower + length].reshape(length ** 3)
    diagonal_block = matmul(basis, apply_box(basis, own_potential, length).T)
    return (basis, diagonal_block)

def pair_block(own_face, other_face):
    return -0.5 * jnp.einsum('xyzac,xyzbc->xyzab', own_face, other_face, precision=lax.Precision.HIGHEST)

def reference(orbitals, potential, coefficients):
    length = EDGE
    grid_x, grid_y, grid_z = (orbitals.shape[0], orbitals.shape[1], orbitals.shape[2])
    spectrum_top = 6.0 + jnp.max(potential)
    centre = (spectrum_top + cutoff) / 2.0
    half_width = (spectrum_top - cutoff) / 2.0
    padded = jnp.pad(potential, ((length, 0), (length, 0), (length, 0)), mode='wrap')
    orbital_flat = orbitals.reshape(grid_x * grid_y * grid_z, orbitals.shape[3], orbitals.shape[4])

    def per_element(index):
        index_x = (index // (grid_y * grid_z)).astype(jnp.int32)
        index_y = (index // grid_z % grid_y).astype(jnp.int32)
        index_z = (index % grid_z).astype(jnp.int32)
        ext_potential = lax.dynamic_slice(padded, (index_x * length, index_y * length, index_z * length), (2 * length, 2 * length, 2 * length))
        return element_basis(orbital_flat[index], ext_potential, length, centre, half_width)
    bases, block_list = lax.map(per_element, jnp.arange(grid_x * grid_y * grid_z, dtype=jnp.int32))
    orbital_count = orbitals.shape[3]
    cube = bases.reshape(grid_x, grid_y, grid_z, orbital_count, length, length, length)
    block_list = block_list.reshape(grid_x, grid_y, grid_z, orbital_count, orbital_count)
    shape_face = (grid_x, grid_y, grid_z, orbital_count, length * length)
    low_x = cube[:, :, :, :, 0, :, :].reshape(shape_face)
    high_x = cube[:, :, :, :, length - 1, :, :].reshape(shape_face)
    low_y = cube[:, :, :, :, :, 0, :].reshape(shape_face)
    high_y = cube[:, :, :, :, :, length - 1, :].reshape(shape_face)
    low_z = cube[:, :, :, :, :, :, 0].reshape(shape_face)
    high_z = cube[:, :, :, :, :, :, length - 1].reshape(shape_face)
    couplings = ((pair_block(low_x, jnp.roll(high_x, 1, axis=0)), 1, 0), (pair_block(high_x, jnp.roll(low_x, -1, axis=0)), -1, 0), (pair_block(low_y, jnp.roll(high_y, 1, axis=1)), 1, 1), (pair_block(high_y, jnp.roll(low_y, -1, axis=1)), -1, 1), (pair_block(low_z, jnp.roll(high_z, 1, axis=2)), 1, 2), (pair_block(high_z, jnp.roll(low_z, -1, axis=2)), -1, 2))

    def galerkin(vectors):
        result = jnp.einsum('xyzab,xyzbc->xyzac', block_list, vectors, precision=lax.Precision.HIGHEST)
        for coupling, amount, axis_index in couplings:
            result = result + jnp.einsum('xyzab,xyzbc->xyzac', coupling, jnp.roll(vectors, amount, axis=axis_index), precision=lax.Precision.HIGHEST)
        return result
    return chebyshev(galerkin, coefficients, DG_STEPS, centre, half_width)
```

```python
import functools
import itertools

import jax
import jax.numpy as jnp
from jax import lax
from jax.experimental import pallas as pl
from jax.experimental.pallas import tpu as pltpu
from jax.sharding import PartitionSpec as P

NEWTON = 6
CUTOFF = 1.0
SHIFT = 4.0
AXES = ("gx", "gy", "gz")
MESH = pl.DeviceIdType.MESH
F32 = jnp.float32
BF16 = jnp.bfloat16
NT = (((1,), (1,)), ((), ()))
NN = (((1,), (0,)), ((), ()))


def iota(shape, dim):
    return lax.broadcasted_iota(jnp.int32, shape, dim)


def split(a):
    high = a.astype(BF16)
    return high, (a - high.astype(F32)).astype(BF16)


def dot(a, b, dims=NN):
    return lax.dot_general(a, b, dims, preferred_element_type=F32)


def dot_full(a, b, dims=NN):
    return lax.dot_general(a, b, dims, precision=lax.Precision.HIGHEST, preferred_element_type=F32)


def dot3(a, b, dims=NN):
    return dot(a[0], b[0], dims) + (dot(a[0], b[1], dims) + dot(a[1], b[0], dims))


def dot2(a, b, dims=NN):
    high, low = split(a)
    return dot(high, b, dims) + dot(low, b, dims)


def dot2r(a, b, dims=NN):
    high, low = split(b)
    return dot(a, high, dims) + dot(a, low, dims)


def flag(condition, dtype=F32):
    return jnp.where(condition, 1.0, 0.0).astype(dtype)


def plane_matrix(width):
    cells = width * width
    row, col = iota((cells, cells), 0), iota((cells, cells), 1)
    gap = row - col
    inside = lax.div(row, width) == lax.div(col, width)
    near = ((jnp.abs(gap) == 1) & inside) | (jnp.abs(gap) == width)
    return (jnp.where(gap == 0, 3.0 - SHIFT, 0.0) - 0.5 * flag(near)).astype(BF16)


def kernel(
    length, sizes, orb_hbm, pot_hbm, coef_hbm, out_ref,
    orb, pot, coef, tiles, max1, max2, wide, u, v, rest, facet, ft_in, v_in, p_out, p_in,
    load_sem, tile_send, tile_recv, m1_send, m1_recv, m2_send, m2_recv,
    v_send, v_recv, f_send, f_recv, p_send, p_recv,
):
    me = [lax.axis_index(a) for a in AXES]
    rows, cols = coef.shape
    doubled, area = 2 * length, length * length
    plane, lower = doubled * doubled, length // 2
    half = cols // 2

    def at(offset):
        return tuple(lax.rem(me[k] + (offset[k] % sizes[k]), sizes[k]) for k in range(3))

    def remote(src, dst, send, recv, offset):
        return pltpu.make_async_remote_copy(
            src_ref=src, dst_ref=dst, send_sem=send, recv_sem=recv, device_id=at(offset), device_id_type=MESH
        )

    tile_slots = [s for s in itertools.product((0, 1), repeat=3) if s != (1, 1, 1)]
    tile_to = {s: tuple(1 - k for k in s) for s in tile_slots}
    first = [(d, 0, 0) for d in range(1, sizes[0])]
    second = [(0, b, c) for b in range(sizes[1]) for c in range(sizes[2])][1:]
    faces = []
    for axis in range(3):
        for side in (-1, 1):
            faces.append(tuple(side if k == axis else 0 for k in range(3)))

    def wrapped(offset):
        return tuple(o % n for o, n in zip(offset, sizes))

    greeted = set()
    for offset in list(tile_to.values()) + first + second + faces:
        greeted.add(wrapped(offset))
        greeted.add(wrapped(tuple(-o for o in offset)))
    greeted = sorted(greeted)

    barrier = pltpu.get_barrier_semaphore()
    for offset in greeted:
        pl.semaphore_signal(barrier, inc=1, device_id=at(offset), device_id_type=MESH)

    load_pot = pltpu.make_async_copy(pot_hbm, pot, load_sem.at[0])
    load_orb = pltpu.make_async_copy(
        orb_hbm.at[:, pl.ds((lower - 2) * plane, (length + 4) * plane)], orb, load_sem.at[1]
    )
    load_coef = pltpu.make_async_copy(coef_hbm, coef, load_sem.at[2])
    load_pot.start()
    load_orb.start()
    load_coef.start()

    load_pot.wait()
    lanes = length * doubled
    flat = pot[...].reshape(area, length)
    spread = flag(lax.rem(iota((length, lanes), 1), doubled) == iota((length, lanes), 0))
    keep = lax.div(iota((area, lanes), 1), doubled) == lax.rem(iota((area, lanes), 0), length)
    spread_rows = jnp.where(keep, dot_full(flat, spread), 0.0)
    own = len(tile_slots)
    tiles[own] = jnp.sum(spread_rows.reshape(length, length, lanes), axis=1)
    top = jnp.max(jnp.max(pot[...], axis=0), axis=(0, 1), keepdims=True)
    max1[0] = jnp.broadcast_to(top, max1.shape[1:])

    pl.semaphore_wait(barrier, len(greeted))

    sends = []
    for d, offset in enumerate(first):
        sends.append(remote(max1.at[0], max1.at[d + 1], m1_send.at[d], m1_recv.at[d], offset))
        sends[-1].start()
    tile_copies = []
    for s, slot in enumerate(tile_slots):
        copy = remote(tiles.at[own], tiles.at[s], tile_send.at[s], tile_recv.at[s], tile_to[slot])
        copy.start()
        tile_copies.append(copy)
    m1_copies = list(sends)
    sends += tile_copies

    matrix = plane_matrix(doubled)
    load_orb.wait()

    def w(i):
        return orb[:, pl.ds(i * plane, plane)]

    for i in range(length + 2):
        u[i] = dot2(w(i + 1), matrix) - 0.5 * (w(i) + w(i + 2))

    for copy in m1_copies:
        copy.wait_recv()
    max2[0] = functools.reduce(jnp.maximum, [max1[d] for d in range(sizes[0])])
    m2_copies = []
    for d, offset in enumerate(second):
        copy = remote(max2.at[0], max2.at[d + 1], m2_send.at[d], m2_recv.at[d], offset)
        copy.start()
        m2_copies.append(copy)
    sends += m2_copies

    for copy in tile_copies:
        copy.wait_recv()
    for a in range(2):
        for b in range(2):
            low, high = tiles[4 * a + 2 * b], tiles[4 * a + 2 * b + 1]
            wide[pl.ds(a * length, length), pl.ds(b * lanes, lanes)] = low + pltpu.roll(high, length, 1)

    def potential(x):
        return wide[pl.ds(x, 1), :]

    for i in range(length + 2):
        u[i] = u[i] + potential(i + lower - 1) * w(i + 1)
    for i in range(length):
        centre_plane = u[i + 1]
        v[i] = dot2(centre_plane, matrix) + potential(i + lower) * centre_plane - 0.5 * (u[i] + u[i + 2])

    for copy in m2_copies:
        copy.wait_recv()
    load_coef.wait()
    v_copies = []
    for f, offset in enumerate(faces):
        copy = remote(coef, v_in.at[f ^ 1], v_send.at[f], v_recv.at[f ^ 1], offset)
        copy.start()
        v_copies.append(copy)
    sends += v_copies

    top = functools.reduce(jnp.maximum, [max2[d] for d in range(sizes[1] * sizes[2])])[0:1, 0:1] + 6.0
    centre = (top + CUTOFF) / 2.0
    width = (top - CUTOFF) / 2.0
    away = centre - SHIFT
    alpha = 2.0 / (width * width)
    beta = -2.0 * away * alpha
    gamma = away * away * alpha - 1.0

    source, target = iota((plane, 2 * area), 0), iota((plane, 2 * area), 1)
    inner = lax.rem(target, area)
    wanted = (lower + lax.div(inner, length)) * doubled + lower + lax.rem(inner, length)
    hit = source == wanted
    select = [flag(hit & (lax.div(target, area) == k), BF16) for k in range(2)]

    def filtered(i):
        return alpha * v[i] + beta * u[i + 1] + gamma * w(i + 2)

    own_rows = []
    for pair in range(length // 2):
        rest[:, pl.ds(pair * 2 * area, 2 * area)] = dot2(filtered(2 * pair), select[0]) + dot2(
            filtered(2 * pair + 1), select[1]
        )
        picked = dot_full(wide[pl.ds(lower + 2 * pair, 1), :], select[0].astype(F32)) + dot_full(
            wide[pl.ds(lower + 2 * pair + 1, 1), :], select[1].astype(F32)
        )
        own_rows.append(picked)
    own_potential = jnp.concatenate(own_rows, axis=1)

    r = rest[...]
    gram = dot_full(r, r, NT)
    cells = length * area
    cell = iota((1, cells), 1)
    around = jnp.zeros_like(r)
    for stride in (area, length, 1):
        coordinate = lax.rem(lax.div(cell, stride), length)
        around = around + flag(coordinate > 0) * pltpu.roll(r, stride, 1)
        around = around + flag(coordinate < length - 1) * pltpu.roll(r, cells - stride, 1)
    boxed = (3.0 + own_potential) * r - 0.5 * around
    energy = dot_full(boxed, r, NT)

    face_cell, wanted_row = iota((6 * area, cells), 1), iota((6 * area, 1), 0)
    face, inner = lax.div(wanted_row, area), lax.rem(wanted_row, area)
    major, minor = lax.div(inner, length), lax.rem(inner, length)
    layer = (length - 1) * lax.rem(face, 2)
    axis = lax.div(face, 2)
    picked_cell = jnp.where(
        axis == 0,
        layer * area + inner,
        jnp.where(axis == 1, major * area + layer * length + minor, major * area + minor * length + layer),
    )
    rest_faces = dot2r(flag(face_cell == picked_cell, BF16), r, NT)

    sigma = jnp.sqrt(jnp.sum(jnp.sum(gram * gram, axis=1, keepdims=True), axis=0, keepdims=True))
    eye = flag(iota((rows, rows), 0) == iota((rows, rows), 1))
    product = gram * (1.0 / sigma)
    inverse = None
    for step in range(NEWTON):
        factor = 1.5 * eye - 0.5 * product
        factor_s = split(factor)
        inverse = factor if inverse is None else dot3(factor_s, split(inverse))
        if step < NEWTON - 1:
            once = dot3(split(product), factor_s)
            product = dot3(split(once), factor_s)
    root = inverse * lax.rsqrt(sigma)
    root_s = split(root)

    rest_faces_s = split(rest_faces)
    facet[...] = dot3(rest_faces_s, root_s, NT)
    f_copies = []
    for f, offset in enumerate(faces):
        copy = remote(
            facet.at[pl.ds(f * area, area), :], ft_in.at[pl.ds((f ^ 1) * area, area), :],
            f_send.at[f], f_recv.at[f ^ 1], offset,
        )
        copy.start()
        f_copies.append(copy)
    sends += f_copies

    facet_s = split(facet[...])
    inverse_width = 1.0 / width
    couple = split((-0.5 * inverse_width) * dot3(root_s, rest_faces_s, NT))
    block = dot3(split(dot3(root_s, split(energy))), root_s, NT)
    diagonal = split(inverse_width * (block - centre * eye))

    prior = coef[...]
    current = dot3(diagonal, split(prior))
    carried = [None] * 6
    for f in range(6):
        v_copies[f ^ 1].wait_recv()
        f_copies[f ^ 1].wait_recv()
        carried[f] = dot3(split(ft_in[pl.ds(f * area, area), :]), split(v_in[f]))
    current = current + dot3(couple, split(jnp.concatenate(carried, axis=0)))

    def send_projected(number, part, vectors):
        p_out[number, part] = dot3(facet_s, split(vectors))
        copies = []
        for f, offset in enumerate(faces):
            here, there = pl.ds(f * area, area), pl.ds((f ^ 1) * area, area)
            copy = remote(
                p_out.at[number, part, here, :], p_in.at[number, part, there, :],
                p_send.at[number, part, f], p_recv.at[number, part, f ^ 1], offset,
            )
            copy.start()
            copies.append(copy)
        return copies

    prior = [prior[:, :half], prior[:, half:]]
    current = [current[:, :half], current[:, half:]]
    flying = [send_projected(0, part, current[part]) for part in range(2)]
    for number in range(2):
        following, next_flying = [], []
        for part in range(2):
            mine = 2.0 * dot3(diagonal, split(current[part])) - prior[part]
            for copy in flying[part]:
                copy.wait_recv()
            sends += flying[part]
            mine = mine + 2.0 * dot3(couple, split(p_in[number, part]))
            following.append(mine)
            if number == 0:
                next_flying.append(send_projected(1, part, mine))
            else:
                out_ref[:, pl.ds(part * half, half)] = mine
        prior, current, flying = current, following, next_flying

    for copy in sends:
        copy.wait_send()


def per_device(sizes, orbitals, potential, coefficients):
    length = potential.shape[0]
    rows, cells = orbitals.shape[-2:]
    cols = coefficients.shape[-1]
    doubled, area = 2 * length, length * length
    plane, lanes = doubled * doubled, length * doubled
    others = sizes[1] * sizes[2]
    dma = pltpu.SemaphoreType.DMA
    result = pl.pallas_call(
        functools.partial(kernel, length, sizes),
        out_shape=jax.ShapeDtypeStruct((rows, cols), F32),
        in_specs=[pl.BlockSpec(memory_space=pl.ANY)] * 3,
        out_specs=pl.BlockSpec(memory_space=pltpu.VMEM),
        scratch_shapes=[
            pltpu.VMEM((rows, (length + 4) * plane), F32),
            pltpu.VMEM((length, length, length), F32),
            pltpu.VMEM((rows, cols), F32),
            pltpu.VMEM((8, length, lanes), F32),
            pltpu.VMEM((sizes[0], 8, 128), F32),
            pltpu.VMEM((others, 8, 128), F32),
            pltpu.VMEM((doubled, plane), F32),
            pltpu.VMEM((length + 2, rows, plane), F32),
            pltpu.VMEM((length, rows, plane), F32),
            pltpu.VMEM((rows, length * area), F32),
            pltpu.VMEM((6 * area, rows), F32),
            pltpu.VMEM((6 * area, rows), F32),
            pltpu.VMEM((6, rows, cols), F32),
            pltpu.VMEM((2, 2, 6 * area, cols // 2), F32),
            pltpu.VMEM((2, 2, 6 * area, cols // 2), F32),
            dma((3,)),
            dma((7,)),
            dma((7,)),
            dma((max(sizes[0] - 1, 1),)),
            dma((max(sizes[0] - 1, 1),)),
            dma((max(others - 1, 1),)),
            dma((max(others - 1, 1),)),
            dma((6,)),
            dma((6,)),
            dma((6,)),
            dma((6,)),
            dma((2, 2, 6)),
            dma((2, 2, 6)),
        ],
        compiler_params=pltpu.CompilerParams(
            collective_id=0, has_side_effects=True, vmem_limit_bytes=40 * 1024 * 1024
        ),
    )(orbitals.reshape(rows, cells), potential, coefficients.reshape(rows, cols))
    return result.reshape(coefficients.shape)


def solution(mesh):
    sizes = tuple(mesh.shape[a] for a in AXES)
    placed = (P("gx", "gy", "gz", None, None), P("gx", "gy", "gz"), P("gx", "gy", "gz", None, None))
    return jax.shard_map(
        functools.partial(per_device, sizes),
        mesh=mesh,
        in_specs=placed,
        out_specs=P("gx", "gy", "gz", None, None),
        check_vma=False,
    )
```

```python
import functools
import itertools

import jax
import jax.numpy as jnp
from jax import lax
from jax.experimental import pallas as pl
from jax.experimental.pallas import tpu as pltpu
from jax.sharding import PartitionSpec as P

NEWTON = 6
CUTOFF = 1.0
SHIFT = 4.0
AXES = ("gx", "gy", "gz")
MESH = pl.DeviceIdType.MESH
F32 = jnp.float32
BF16 = jnp.bfloat16
NT = (((1,), (1,)), ((), ()))
NN = (((1,), (0,)), ((), ()))


def iota(shape, dim):
    return lax.broadcasted_iota(jnp.int32, shape, dim)


def split(a):
    high = a.astype(BF16)
    return high, (a - high.astype(F32)).astype(BF16)


def dot(a, b, dims=NN):
    return lax.dot_general(a, b, dims, preferred_element_type=F32)


def dot_full(a, b, dims=NN):
    return lax.dot_general(a, b, dims, precision=lax.Precision.HIGHEST, preferred_element_type=F32)


def dot3(a, b, dims=NN):
    rows = a[0].shape[0]
    both = dot(jnp.concatenate(a, axis=0), b[0], dims)
    return both[:rows] + (both[rows:] + dot(a[0], b[1], dims))


def dot2(a, b, dims=NN):
    rows = a.shape[0]
    both = dot(jnp.concatenate(split(a), axis=0), b, dims)
    return both[:rows] + both[rows:]


def dot2r(a, b, dims=NN):
    high, low = split(b)
    return dot(a, high, dims) + dot(a, low, dims)


def flag(condition, dtype=F32):
    return jnp.where(condition, 1.0, 0.0).astype(dtype)


def plane_matrix(width):
    cells = width * width
    row, col = iota((cells, cells), 0), iota((cells, cells), 1)
    gap = row - col
    inside = lax.div(row, width) == lax.div(col, width)
    near = ((jnp.abs(gap) == 1) & inside) | (jnp.abs(gap) == width)
    return (jnp.where(gap == 0, 3.0 - SHIFT, 0.0) - 0.5 * flag(near)).astype(BF16)


def kernel(
    length, sizes, orb_hbm, pot_hbm, coef_hbm, out_ref,
    matrix, select, pick, orb, pot, coef, tiles, max1, max2, wide, u, v, rest, facet, ft_in, v_in, p_out, p_in,
    load_sem, tile_send, tile_recv, m1_send, m1_recv, m2_send, m2_recv,
    v_send, v_recv, f_send, f_recv, p_send, p_recv,
):
    me = [lax.axis_index(a) for a in AXES]
    rows, cols = coef.shape
    doubled, area = 2 * length, length * length
    plane, lower = doubled * doubled, length // 2
    half = cols // 2

    def at(offset):
        return tuple(lax.rem(me[k] + (offset[k] % sizes[k]), sizes[k]) for k in range(3))

    def remote(src, dst, send, recv, offset):
        return pltpu.make_async_remote_copy(
            src_ref=src, dst_ref=dst, send_sem=send, recv_sem=recv, device_id=at(offset), device_id_type=MESH
        )

    tile_slots = [s for s in itertools.product((0, 1), repeat=3) if s != (1, 1, 1)]
    tile_to = {s: tuple(1 - k for k in s) for s in tile_slots}
    first = [(d, 0, 0) for d in range(1, sizes[0])]
    second = [(0, b, c) for b in range(sizes[1]) for c in range(sizes[2])][1:]
    faces = []
    for axis in range(3):
        for side in (-1, 1):
            faces.append(tuple(side if k == axis else 0 for k in range(3)))

    def wrapped(offset):
        return tuple(o % n for o, n in zip(offset, sizes))

    greeted = set()
    for offset in list(tile_to.values()) + first + second + faces:
        greeted.add(wrapped(offset))
        greeted.add(wrapped(tuple(-o for o in offset)))
    greeted = sorted(greeted)

    barrier = pltpu.get_barrier_semaphore()
    for offset in greeted:
        pl.semaphore_signal(barrier, inc=1, device_id=at(offset), device_id_type=MESH)

    load_pot = pltpu.make_async_copy(pot_hbm, pot, load_sem.at[0])
    load_orb = pltpu.make_async_copy(
        orb_hbm.at[:, pl.ds((lower - 2) * plane, (length + 4) * plane)], orb, load_sem.at[1]
    )
    load_coef = pltpu.make_async_copy(coef_hbm, coef, load_sem.at[2])
    load_pot.start()
    load_orb.start()
    load_coef.start()

    matrix[...] = plane_matrix(doubled)
    source, target = iota((plane, 2 * area), 0), iota((plane, 2 * area), 1)
    inner = lax.rem(target, area)
    wanted = (lower + lax.div(inner, length)) * doubled + lower + lax.rem(inner, length)
    for k in range(2):
        select[k] = flag((source == wanted) & (lax.div(target, area) == k), BF16)
    cells = length * area
    cell = iota((1, cells), 1)
    for f in range(6):
        inner = iota((area, 1), 0)
        major, minor = lax.div(inner, length), lax.rem(inner, length)
        layer = (length - 1) * (f % 2)
        picked_cell = (
            layer * area + inner, major * area + layer * length + minor, major * area + minor * length + layer
        )[f // 2]
        pick[pl.ds(f * area, area), :] = flag(iota((area, cells), 1) == picked_cell, BF16)

    load_pot.wait()
    lanes = length * doubled
    flat = pot[...].reshape(area, length)
    spread = flag(lax.rem(iota((length, lanes), 1), doubled) == iota((length, lanes), 0))
    keep = lax.div(iota((area, lanes), 1), doubled) == lax.rem(iota((area, lanes), 0), length)
    spread_rows = jnp.where(keep, dot_full(flat, spread), 0.0)
    own = len(tile_slots)
    tiles[own] = jnp.sum(spread_rows.reshape(length, length, lanes), axis=1)
    top = jnp.max(jnp.max(pot[...], axis=0), axis=(0, 1), keepdims=True)
    max1[0] = jnp.broadcast_to(top, max1.shape[1:])

    pl.semaphore_wait(barrier, len(greeted))

    sends = []
    for d, offset in enumerate(first):
        sends.append(remote(max1.at[0], max1.at[d + 1], m1_send.at[d], m1_recv.at[d], offset))
        sends[-1].start()
    tile_copies = []
    for s, slot in enumerate(tile_slots):
        copy = remote(tiles.at[own], tiles.at[s], tile_send.at[s], tile_recv.at[s], tile_to[slot])
        copy.start()
        tile_copies.append(copy)
    m1_copies = list(sends)
    sends += tile_copies

    load_coef.wait()
    v_copies = {}
    shared = [f for f in range(6) if f % 2 == 0 or sizes[f // 2] > 2]
    for f in shared:
        v_copies[f] = remote(coef, v_in.at[f ^ 1], v_send.at[f], v_recv.at[f ^ 1], faces[f])
    for f in shared[:2]:
        v_copies[f].start()
    sends += v_copies.values()

    load_orb.wait()

    def w(i):
        return orb[:, pl.ds(i * plane, plane)]

    for i in range(length + 2):
        u[i] = dot2(w(i + 1), matrix[...]) - 0.5 * (w(i) + w(i + 2))

    for copy in m1_copies:
        copy.wait_recv()
    max2[0] = functools.reduce(jnp.maximum, [max1[d] for d in range(sizes[0])])
    m2_copies = []
    for d, offset in enumerate(second):
        copy = remote(max2.at[0], max2.at[d + 1], m2_send.at[d], m2_recv.at[d], offset)
        copy.start()
        m2_copies.append(copy)
    sends += m2_copies

    for copy in tile_copies:
        copy.wait_recv()
    for a in range(2):
        for b in range(2):
            low, high = tiles[4 * a + 2 * b], tiles[4 * a + 2 * b + 1]
            wide[pl.ds(a * length, length), pl.ds(b * lanes, lanes)] = low + pltpu.roll(high, length, 1)

    def potential(x):
        return wide[pl.ds(x, 1), :]

    for i in range(length + 2):
        u[i] = u[i] + potential(i + lower - 1) * w(i + 1)
    for i in range(length):
        centre_plane = u[i + 1]
        v[i] = dot2(centre_plane, matrix[...]) + potential(i + lower) * centre_plane - 0.5 * (u[i] + u[i + 2])

    for copy in m2_copies:
        copy.wait_recv()
    for f in shared[2:]:
        v_copies[f].start()

    top = functools.reduce(jnp.maximum, [max2[d] for d in range(sizes[1] * sizes[2])])[0:1, 0:1] + 6.0
    centre = (top + CUTOFF) / 2.0
    width = (top - CUTOFF) / 2.0
    away = centre - SHIFT
    alpha = 2.0 / (width * width)
    beta = -2.0 * away * alpha
    gamma = away * away * alpha - 1.0

    def filtered(i):
        return alpha * v[i] + beta * u[i + 1] + gamma * w(i + 2)

    own_rows = []
    for pair in range(length // 2):
        rest[:, pl.ds(pair * 2 * area, 2 * area)] = dot2(filtered(2 * pair), select[0]) + dot2(
            filtered(2 * pair + 1), select[1]
        )
        picked = dot_full(wide[pl.ds(lower + 2 * pair, 1), :], select[0].astype(F32)) + dot_full(
            wide[pl.ds(lower + 2 * pair + 1, 1), :], select[1].astype(F32)
        )
        own_rows.append(picked)
    own_potential = jnp.concatenate(own_rows, axis=1)

    r = rest[...]
    gram = dot_full(r, r, NT)
    sigma = jnp.sqrt(jnp.sum(jnp.sum(gram * gram, axis=1, keepdims=True), axis=0, keepdims=True))
    eye = flag(iota((rows, rows), 0) == iota((rows, rows), 1))
    product = gram * (1.0 / sigma)
    inverse = None
    r_s = split(r)
    rest_faces = []
    for step in range(NEWTON):
        for f in range(6 * step // NEWTON, 6 * (step + 1) // NEWTON):
            here = pick[pl.ds(f * area, area), :]
            rest_faces.append(dot(here, r_s[0], NT) + dot(here, r_s[1], NT))
        factor = 1.5 * eye - 0.5 * product
        factor_s = split(factor)
        inverse = factor if inverse is None else dot3(factor_s, split(inverse))
        if step < NEWTON - 1:
            once = dot3(split(product), factor_s)
            product = dot3(split(once), factor_s)
    root = inverse * lax.rsqrt(sigma)
    root_s = split(root)

    rest_faces_s = split(jnp.concatenate(rest_faces, axis=0))
    facet[...] = dot3(rest_faces_s, root_s, NT)
    f_copies = []
    for f, offset in enumerate(faces):
        copy = remote(
            facet.at[pl.ds(f * area, area), :], ft_in.at[pl.ds((f ^ 1) * area, area), :],
            f_send.at[f], f_recv.at[f ^ 1], offset,
        )
        copy.start()
        f_copies.append(copy)
    sends += f_copies

    facet_s = split(facet[...])
    inverse_width = 1.0 / width
    couple = split((-0.5 * inverse_width) * dot3(root_s, rest_faces_s, NT))
    around = jnp.zeros_like(r)
    for stride in (area, length, 1):
        coordinate = lax.rem(lax.div(cell, stride), length)
        around = around + flag(coordinate > 0) * pltpu.roll(r, stride, 1)
        around = around + flag(coordinate < length - 1) * pltpu.roll(r, cells - stride, 1)
    boxed = (3.0 + own_potential) * r - 0.5 * around
    energy = dot3(split(boxed), r_s, NT)
    block = dot3(split(dot3(root_s, split(energy))), root_s, NT)
    diagonal = split(inverse_width * (block - centre * eye))

    prior = coef[...]
    current = dot3(diagonal, split(prior))
    for copy in v_copies.values():
        copy.wait_recv()
    came = [split(v_in[f if f ^ 1 in shared else f ^ 1]) for f in range(6)]
    carried = []
    for f in range(6):
        f_copies[f ^ 1].wait_recv()
        carried.append(dot3(split(ft_in[pl.ds(f * area, area), :]), came[f]))
    current = current + dot3(couple, split(jnp.concatenate(carried, axis=0)))

    def send_projected(number, part, vectors):
        p_out[number, part] = dot3(facet_s, split(vectors))
        copies = []
        for f, offset in enumerate(faces):
            here, there = pl.ds(f * area, area), pl.ds((f ^ 1) * area, area)
            copy = remote(
                p_out.at[number, part, here, :], p_in.at[number, part, there, :],
                p_send.at[number, part, f], p_recv.at[number, part, f ^ 1], offset,
            )
            copy.start()
            copies.append(copy)
        return copies

    prior = [prior[:, :half], prior[:, half:]]
    current = [current[:, :half], current[:, half:]]
    flying = [send_projected(0, part, current[part]) for part in range(2)]
    for number in range(2):
        following, next_flying = [], []
        for part in range(2):
            mine = 2.0 * dot3(diagonal, split(current[part])) - prior[part]
            for copy in flying[part]:
                copy.wait_recv()
            sends += flying[part]
            mine = mine + 2.0 * dot3(couple, split(p_in[number, part]))
            following.append(mine)
            if number == 0:
                next_flying.append(send_projected(1, part, mine))
            else:
                out_ref[:, pl.ds(part * half, half)] = mine
        prior, current, flying = current, following, next_flying

    for copy in sends:
        copy.wait_send()


def per_device(sizes, orbitals, potential, coefficients):
    length = potential.shape[0]
    rows, cells = orbitals.shape[-2:]
    cols = coefficients.shape[-1]
    doubled, area = 2 * length, length * length
    plane, lanes = doubled * doubled, length * doubled
    others = sizes[1] * sizes[2]
    dma = pltpu.SemaphoreType.DMA
    result = pl.pallas_call(
        functools.partial(kernel, length, sizes),
        out_shape=jax.ShapeDtypeStruct((rows, cols), F32),
        in_specs=[pl.BlockSpec(memory_space=pltpu.HBM)] * 3,
        out_specs=pl.BlockSpec(memory_space=pltpu.VMEM),
        scratch_shapes=[
            pltpu.VMEM((plane, plane), BF16),
            pltpu.VMEM((2, plane, 2 * area), BF16),
            pltpu.VMEM((6 * area, length * area), BF16),
            pltpu.VMEM((rows, (length + 4) * plane), F32),
            pltpu.VMEM((length, length, length), F32),
            pltpu.VMEM((rows, cols), F32),
            pltpu.VMEM((8, length, lanes), F32),
            pltpu.VMEM((sizes[0], 8, 128), F32),
            pltpu.VMEM((others, 8, 128), F32),
            pltpu.VMEM((doubled, plane), F32),
            pltpu.VMEM((length + 2, rows, plane), F32),
            pltpu.VMEM((length, rows, plane), F32),
            pltpu.VMEM((rows, length * area), F32),
            pltpu.VMEM((6 * area, rows), F32),
            pltpu.VMEM((6 * area, rows), F32),
            pltpu.VMEM((6, rows, cols), F32),
            pltpu.VMEM((2, 2, 6 * area, cols // 2), F32),
            pltpu.VMEM((2, 2, 6 * area, cols // 2), F32),
            dma((3,)),
            dma((7,)),
            dma((7,)),
            dma((max(sizes[0] - 1, 1),)),
            dma((max(sizes[0] - 1, 1),)),
            dma((max(others - 1, 1),)),
            dma((max(others - 1, 1),)),
            dma((6,)),
            dma((6,)),
            dma((6,)),
            dma((6,)),
            dma((2, 2, 6)),
            dma((2, 2, 6)),
        ],
        compiler_params=pltpu.CompilerParams(
            collective_id=0, has_side_effects=True, vmem_limit_bytes=60 * 1024 * 1024
        ),
    )(orbitals.reshape(rows, cells), potential, coefficients.reshape(rows, cols))
    return result.reshape(coefficients.shape)


def solution(mesh):
    sizes = tuple(mesh.shape[a] for a in AXES)
    placed = (P("gx", "gy", "gz", None, None), P("gx", "gy", "gz"), P("gx", "gy", "gz", None, None))
    return jax.shard_map(
        functools.partial(per_device, sizes),
        mesh=mesh,
        in_specs=placed,
        out_specs=P("gx", "gy", "gz", None, None),
        check_vma=False,
    )
```

```python
import functools
import itertools

import jax
import jax.numpy as jnp
from jax import lax
from jax.experimental import pallas as pl
from jax.experimental.pallas import tpu as pltpu
from jax.sharding import PartitionSpec as P

NEWTON = 6
PARTS = 1
CUTOFF = 1.0
SHIFT = 4.0
AXES = ("gx", "gy", "gz")
MESH = pl.DeviceIdType.MESH
F32 = jnp.float32
BF16 = jnp.bfloat16
NT = (((1,), (1,)), ((), ()))
NN = (((1,), (0,)), ((), ()))


def iota(shape, dim):
    return lax.broadcasted_iota(jnp.int32, shape, dim)


def split(a):
    high = a.astype(BF16)
    return high, (a - high.astype(F32)).astype(BF16)


def dot(a, b, dims=NN):
    return lax.dot_general(a, b, dims, preferred_element_type=F32)


def dot_full(a, b, dims=NN):
    return lax.dot_general(a, b, dims, precision=lax.Precision.HIGHEST, preferred_element_type=F32)


def dot3(a, b, dims=NN):
    rows = a[0].shape[0]
    both = dot(jnp.concatenate(a, axis=0), b[0], dims)
    return both[:rows] + (both[rows:] + dot(a[0], b[1], dims))


def dot2(a, b, dims=NN):
    rows = a.shape[0]
    both = dot(jnp.concatenate(split(a), axis=0), b, dims)
    return both[:rows] + both[rows:]


def dot2r(a, b, dims=NN):
    high, low = split(b)
    return dot(a, high, dims) + dot(a, low, dims)


def flag(condition, dtype=F32):
    return jnp.where(condition, 1.0, 0.0).astype(dtype)


def plane_matrix(width):
    cells = width * width
    row, col = iota((cells, 1), 0), iota((1, cells), 1)
    gap = row - col
    inside = lax.div(row, width) == lax.div(col, width)
    near = ((jnp.abs(gap) == 1) & inside) | (jnp.abs(gap) == width)
    return (jnp.where(gap == 0, 3.0 - SHIFT, 0.0) - 0.5 * flag(near)).astype(BF16)


def kernel(
    length, sizes, orb_hbm, pot_hbm, coef_hbm, out_ref,
    matrix, select, pick, orb, pot, coef, tiles, max1, max2, wide, u, v, rest, facet, ft_in, v_in, p_out, p_in,
    load_sem, tile_send, tile_recv, m1_send, m1_recv, m2_send, m2_recv,
    v_send, v_recv, f_send, f_recv, p_send, p_recv,
):
    me = [lax.axis_index(a) for a in AXES]
    rows, cols = coef.shape
    doubled, area = 2 * length, length * length
    plane, lower = doubled * doubled, length // 2
    half = cols // PARTS

    def at(offset):
        return tuple(lax.rem(me[k] + (offset[k] % sizes[k]), sizes[k]) for k in range(3))

    def remote(src, dst, send, recv, offset):
        return pltpu.make_async_remote_copy(
            src_ref=src, dst_ref=dst, send_sem=send, recv_sem=recv, device_id=at(offset), device_id_type=MESH
        )

    tile_slots = [s for s in itertools.product((0, 1), repeat=3) if s != (1, 1, 1)]
    tile_to = {s: tuple(1 - k for k in s) for s in tile_slots}
    first = [(d, 0, 0) for d in range(1, sizes[0])]
    second = [(0, b, c) for b in range(sizes[1]) for c in range(sizes[2])][1:]
    faces = []
    for axis in range(3):
        for side in (-1, 1):
            faces.append(tuple(side if k == axis else 0 for k in range(3)))

    def wrapped(offset):
        return tuple(o % n for o, n in zip(offset, sizes))

    greeted = set()
    for offset in list(tile_to.values()) + first + second + faces:
        greeted.add(wrapped(offset))
        greeted.add(wrapped(tuple(-o for o in offset)))
    greeted = sorted(greeted)

    barrier = pltpu.get_barrier_semaphore()
    for offset in greeted:
        pl.semaphore_signal(barrier, inc=1, device_id=at(offset), device_id_type=MESH)

    load_pot = pltpu.make_async_copy(pot_hbm, pot, load_sem.at[0])
    load_orb = pltpu.make_async_copy(
        orb_hbm.at[:, pl.ds((lower - 2) * plane, (length + 4) * plane)], orb, load_sem.at[1]
    )
    load_coef = pltpu.make_async_copy(coef_hbm, coef, load_sem.at[2])
    load_pot.start()
    load_orb.start()
    load_coef.start()

    matrix[...] = plane_matrix(doubled)
    source, target = iota((plane, 1), 0), iota((1, 2 * area), 1)
    inner = lax.rem(target, area)
    wanted = (lower + lax.div(inner, length)) * doubled + lower + lax.rem(inner, length)
    for k in range(2):
        select[k] = flag(source == jnp.where(lax.div(target, area) == k, wanted, -1), BF16)
    cells = length * area
    cell = iota((1, cells), 1)
    for f in range(6):
        inner = iota((area, 1), 0)
        major, minor = lax.div(inner, length), lax.rem(inner, length)
        layer = (length - 1) * (f % 2)
        picked_cell = (
            layer * area + inner, major * area + layer * length + minor, major * area + minor * length + layer
        )[f // 2]
        pick[pl.ds(f * area, area), :] = flag(cell == picked_cell, BF16)

    load_pot.wait()
    lanes = length * doubled
    flat = pot[...].reshape(area, length)
    spread = flag(lax.rem(iota((1, lanes), 1), doubled) == iota((length, 1), 0))
    keep = lax.div(iota((1, lanes), 1), doubled) == lax.rem(iota((area, 1), 0), length)
    spread_rows = jnp.where(keep, dot_full(flat, spread), 0.0)
    own = len(tile_slots)
    tiles[own] = jnp.sum(spread_rows.reshape(length, length, lanes), axis=1)
    top = jnp.max(jnp.max(pot[...], axis=0), axis=(0, 1), keepdims=True)
    max1[0] = jnp.broadcast_to(top, max1.shape[1:])

    pl.semaphore_wait(barrier, len(greeted))

    sends = []
    for d, offset in enumerate(first):
        sends.append(remote(max1.at[0], max1.at[d + 1], m1_send.at[d], m1_recv.at[d], offset))
        sends[-1].start()
    tile_copies = []
    for s, slot in enumerate(tile_slots):
        copy = remote(tiles.at[own], tiles.at[s], tile_send.at[s], tile_recv.at[s], tile_to[slot])
        copy.start()
        tile_copies.append(copy)
    m1_copies = list(sends)
    sends += tile_copies

    load_coef.wait()
    v_copies = {}
    shared = [f for f in range(6) if f % 2 == 0 or sizes[f // 2] > 2]
    for f in shared:
        v_copies[f] = remote(coef, v_in.at[f ^ 1], v_send.at[f], v_recv.at[f ^ 1], faces[f])
    for f in shared[:2]:
        v_copies[f].start()
    sends += v_copies.values()

    load_orb.wait()

    def w(i):
        return orb[:, pl.ds(i * plane, plane)]

    for i in range(length + 2):
        u[i] = dot2(w(i + 1), matrix[...]) - 0.5 * (w(i) + w(i + 2))

    for copy in m1_copies:
        copy.wait_recv()
    max2[0] = functools.reduce(jnp.maximum, [max1[d] for d in range(sizes[0])])
    m2_copies = []
    for d, offset in enumerate(second):
        copy = remote(max2.at[0], max2.at[d + 1], m2_send.at[d], m2_recv.at[d], offset)
        copy.start()
        m2_copies.append(copy)
    sends += m2_copies

    for copy in tile_copies:
        copy.wait_recv()
    for a in range(2):
        for b in range(2):
            low, high = tiles[4 * a + 2 * b], tiles[4 * a + 2 * b + 1]
            wide[pl.ds(a * length, length), pl.ds(b * lanes, lanes)] = low + pltpu.roll(high, length, 1)

    def potential(x):
        return wide[pl.ds(x, 1), :]

    for i in range(length + 2):
        u[i] = u[i] + potential(i + lower - 1) * w(i + 1)
    for i in range(length):
        centre_plane = u[i + 1]
        v[i] = dot2(centre_plane, matrix[...]) + potential(i + lower) * centre_plane - 0.5 * (u[i] + u[i + 2])

    for copy in m2_copies:
        copy.wait_recv()
    for f in shared[2:]:
        v_copies[f].start()

    top = functools.reduce(jnp.maximum, [max2[d] for d in range(sizes[1] * sizes[2])])[0:1, 0:1] + 6.0
    centre = (top + CUTOFF) / 2.0
    width = (top - CUTOFF) / 2.0
    away = centre - SHIFT
    alpha = 2.0 / (width * width)
    beta = -2.0 * away * alpha
    gamma = away * away * alpha - 1.0

    def filtered(i):
        return alpha * v[i] + beta * u[i + 1] + gamma * w(i + 2)

    own_rows = []
    for pair in range(length // 2):
        rest[:, pl.ds(pair * 2 * area, 2 * area)] = dot2(filtered(2 * pair), select[0]) + dot2(
            filtered(2 * pair + 1), select[1]
        )
        picked = dot_full(wide[pl.ds(lower + 2 * pair, 1), :], select[0].astype(F32)) + dot_full(
            wide[pl.ds(lower + 2 * pair + 1, 1), :], select[1].astype(F32)
        )
        own_rows.append(picked)
    own_potential = jnp.concatenate(own_rows, axis=1)

    r = rest[...]
    gram = dot_full(r, r, NT)
    sigma = jnp.sqrt(jnp.sum(jnp.sum(gram * gram, axis=1, keepdims=True), axis=0, keepdims=True))
    eye = flag(iota((rows, rows), 0) == iota((rows, rows), 1))
    product = gram * (1.0 / sigma)
    inverse = None
    r_s = split(r)
    rest_faces = []
    for step in range(NEWTON):
        for f in range(6 * step // NEWTON, 6 * (step + 1) // NEWTON):
            here = pick[pl.ds(f * area, area), :]
            rest_faces.append(dot(here, r_s[0], NT) + dot(here, r_s[1], NT))
        factor = 1.5 * eye - 0.5 * product
        factor_s = split(factor)
        inverse = factor if inverse is None else dot3(factor_s, split(inverse))
        if step < NEWTON - 1:
            once = dot3(split(product), factor_s)
            product = dot3(split(once), factor_s)
    root = inverse * lax.rsqrt(sigma)
    root_s = split(root)

    rest_faces_s = split(jnp.concatenate(rest_faces, axis=0))
    facet[...] = dot3(rest_faces_s, root_s, NT)
    f_copies = []
    face_copies = []
    for f, offset in enumerate(faces):
        if sizes[f // 2] > 2:
            face_copies.append((f, pl.ds(f * area, area), pl.ds((f ^ 1) * area, area), offset))
        elif f % 2 == 0:
            both = pl.ds(f * area, 2 * area)
            face_copies.append((f, both, both, offset))
    for f, here, there, offset in face_copies:
        copy = remote(facet.at[here, :], ft_in.at[there, :], f_send.at[f], f_recv.at[f], offset)
        copy.start()
        f_copies.append(copy)
    sends += f_copies

    facet_s = split(facet[...])
    inverse_width = 1.0 / width
    slots = []
    for f in range(6):
        slots.append(rest_faces[f if sizes[f // 2] > 2 else f ^ 1])
    slots_s = split(jnp.concatenate(slots, axis=0))
    couple = split((-0.5 * inverse_width) * dot3(root_s, slots_s, NT))
    around = jnp.zeros_like(r)
    for stride in (area, length, 1):
        coordinate = lax.rem(lax.div(cell, stride), length)
        around = around + flag(coordinate > 0) * pltpu.roll(r, stride, 1)
        around = around + flag(coordinate < length - 1) * pltpu.roll(r, cells - stride, 1)
    boxed = (3.0 + own_potential) * r - 0.5 * around
    energy = dot3(split(boxed), r_s, NT)
    block = dot3(split(dot3(root_s, split(energy))), root_s, NT)
    diagonal = split(inverse_width * (block - centre * eye))

    prior = coef[...]
    current = dot3(diagonal, split(prior))
    for copy in v_copies.values():
        copy.wait_recv()
    came = [split(v_in[f if f ^ 1 in shared else f ^ 1]) for f in range(6)]
    carried = []
    for copy in f_copies:
        copy.wait_recv()
    for f in range(6):
        carried.append(dot3(split(ft_in[pl.ds(f * area, area), :]), came[f]))
    current = current + dot3(couple, split(jnp.concatenate(carried, axis=0)))

    def send_projected(number, part, vectors):
        p_out[number, part] = dot3(facet_s, split(vectors))
        copies = []
        for f, here, there, offset in face_copies:
            copy = remote(
                p_out.at[number, part, here, :], p_in.at[number, part, there, :],
                p_send.at[number, part, f], p_recv.at[number, part, f], offset,
            )
            copy.start()
            copies.append(copy)
        return copies

    prior = [prior[:, k * half : (k + 1) * half] for k in range(PARTS)]
    current = [current[:, k * half : (k + 1) * half] for k in range(PARTS)]
    flying = [send_projected(0, part, current[part]) for part in range(PARTS)]
    for number in range(2):
        following, next_flying = [], []
        for part in range(PARTS):
            mine = 2.0 * dot3(diagonal, split(current[part])) - prior[part]
            for copy in flying[part]:
                copy.wait_recv()
            sends += flying[part]
            mine = mine + 2.0 * dot3(couple, split(p_in[number, part]))
            following.append(mine)
            if number == 0:
                next_flying.append(send_projected(1, part, mine))
            else:
                out_ref[:, pl.ds(part * half, half)] = mine
        prior, current, flying = current, following, next_flying

    for copy in sends:
        copy.wait_send()


def per_device(sizes, orbitals, potential, coefficients):
    length = potential.shape[0]
    rows, cells = orbitals.shape[-2:]
    cols = coefficients.shape[-1]
    doubled, area = 2 * length, length * length
    plane, lanes = doubled * doubled, length * doubled
    others = sizes[1] * sizes[2]
    dma = pltpu.SemaphoreType.DMA
    result = pl.pallas_call(
        functools.partial(kernel, length, sizes),
        out_shape=jax.ShapeDtypeStruct((rows, cols), F32),
        in_specs=[pl.BlockSpec(memory_space=pltpu.HBM)] * 3,
        out_specs=pl.BlockSpec(memory_space=pltpu.VMEM),
        scratch_shapes=[
            pltpu.VMEM((plane, plane), BF16),
            pltpu.VMEM((2, plane, 2 * area), BF16),
            pltpu.VMEM((6 * area, length * area), BF16),
            pltpu.VMEM((rows, (length + 4) * plane), F32),
            pltpu.VMEM((length, length, length), F32),
            pltpu.VMEM((rows, cols), F32),
            pltpu.VMEM((8, length, lanes), F32),
            pltpu.VMEM((sizes[0], 8, 128), F32),
            pltpu.VMEM((others, 8, 128), F32),
            pltpu.VMEM((doubled, plane), F32),
            pltpu.VMEM((length + 2, rows, plane), F32),
            pltpu.VMEM((length, rows, plane), F32),
            pltpu.VMEM((rows, length * area), F32),
            pltpu.VMEM((6 * area, rows), F32),
            pltpu.VMEM((6 * area, rows), F32),
            pltpu.VMEM((6, rows, cols), F32),
            pltpu.VMEM((2, PARTS, 6 * area, cols // PARTS), F32),
            pltpu.VMEM((2, PARTS, 6 * area, cols // PARTS), F32),
            dma((3,)),
            dma((7,)),
            dma((7,)),
            dma((max(sizes[0] - 1, 1),)),
            dma((max(sizes[0] - 1, 1),)),
            dma((max(others - 1, 1),)),
            dma((max(others - 1, 1),)),
            dma((6,)),
            dma((6,)),
            dma((6,)),
            dma((6,)),
            dma((2, PARTS, 6)),
            dma((2, PARTS, 6)),
        ],
        compiler_params=pltpu.CompilerParams(
            collective_id=0, has_side_effects=True, vmem_limit_bytes=60 * 1024 * 1024
        ),
    )(orbitals.reshape(rows, cells), potential, coefficients.reshape(rows, cols))
    return result.reshape(coefficients.shape)


def solution(mesh):
    sizes = tuple(mesh.shape[a] for a in AXES)
    placed = (P("gx", "gy", "gz", None, None), P("gx", "gy", "gz"), P("gx", "gy", "gz", None, None))
    return jax.shard_map(
        functools.partial(per_device, sizes),
        mesh=mesh,
        in_specs=placed,
        out_specs=P("gx", "gy", "gz", None, None),
        check_vma=False,
    )
```

```python
import functools
import itertools

import jax
import jax.numpy as jnp
from jax import lax
from jax.experimental import pallas as pl
from jax.experimental.pallas import tpu as pltpu
from jax.sharding import PartitionSpec as P

NEWTON = 6
PARTS = 1
CUTOFF = 1.0
SHIFT = 4.0
AXES = ("gx", "gy", "gz")
MESH = pl.DeviceIdType.MESH
F32 = jnp.float32
BF16 = jnp.bfloat16
NT = (((1,), (1,)), ((), ()))
NN = (((1,), (0,)), ((), ()))


def iota(shape, dim):
    return lax.broadcasted_iota(jnp.int32, shape, dim)


def split(a):
    high = a.astype(BF16)
    return high, (a - high.astype(F32)).astype(BF16)


def dot(a, b, dims=NN):
    return lax.dot_general(a, b, dims, preferred_element_type=F32)


def dot_full(a, b, dims=NN):
    return lax.dot_general(a, b, dims, precision=lax.Precision.HIGHEST, preferred_element_type=F32)


def dot3(a, b, dims=NN):
    rows = a[0].shape[0]
    both = dot(jnp.concatenate(a, axis=0), b[0], dims)
    return both[:rows] + (both[rows:] + dot(a[0], b[1], dims))


def dot2(a, b, dims=NN):
    rows = a.shape[0]
    both = dot(jnp.concatenate(split(a), axis=0), b, dims)
    return both[:rows] + both[rows:]


def dot2r(a, b, dims=NN):
    high, low = split(b)
    return dot(a, high, dims) + dot(a, low, dims)


def flag(condition, dtype=F32):
    return jnp.where(condition, 1.0, 0.0).astype(dtype)


def plane_matrix(width):
    cells = width * width
    row, col = iota((cells, 1), 0), iota((1, cells), 1)
    gap = row - col
    inside = lax.div(row, width) == lax.div(col, width)
    near = ((jnp.abs(gap) == 1) & inside) | (jnp.abs(gap) == width)
    return (jnp.where(gap == 0, 3.0 - SHIFT, 0.0) - 0.5 * flag(near)).astype(BF16)


def kernel(
    length, sizes, orb_hbm, pot_hbm, coef_hbm, out_ref,
    matrix, select, pick, orb, pot, coef, tiles, max1, max2, wide, u, v, rest, rest_faces, facet, ft_in, v_in, p_out, p_in,
    load_sem, tile_send, tile_recv, m1_send, m1_recv, m2_send, m2_recv,
    v_send, v_recv, f_send, f_recv, p_send, p_recv,
):
    me = [lax.axis_index(a) for a in AXES]
    rows, cols = coef.shape
    doubled, area = 2 * length, length * length
    plane, lower = doubled * doubled, length // 2
    half = cols // PARTS

    def at(offset):
        return tuple(lax.rem(me[k] + (offset[k] % sizes[k]), sizes[k]) for k in range(3))

    def remote(src, dst, send, recv, offset):
        return pltpu.make_async_remote_copy(
            src_ref=src, dst_ref=dst, send_sem=send, recv_sem=recv, device_id=at(offset), device_id_type=MESH
        )

    tile_slots = [s for s in itertools.product((0, 1), repeat=3) if s != (1, 1, 1)]
    tile_to = {s: tuple(1 - k for k in s) for s in tile_slots}
    first = [(d, 0, 0) for d in range(1, sizes[0])]
    second = [(0, b, c) for b in range(sizes[1]) for c in range(sizes[2])][1:]
    faces = []
    for axis in range(3):
        for side in (-1, 1):
            faces.append(tuple(side if k == axis else 0 for k in range(3)))

    def wrapped(offset):
        return tuple(o % n for o, n in zip(offset, sizes))

    greeted = set()
    for offset in list(tile_to.values()) + first + second + faces:
        greeted.add(wrapped(offset))
        greeted.add(wrapped(tuple(-o for o in offset)))
    greeted = sorted(greeted)

    barrier = pltpu.get_barrier_semaphore()
    for offset in greeted:
        pl.semaphore_signal(barrier, inc=1, device_id=at(offset), device_id_type=MESH)

    load_pot = pltpu.make_async_copy(pot_hbm, pot, load_sem.at[0])
    load_orb = pltpu.make_async_copy(
        orb_hbm.at[:, pl.ds((lower - 2) * plane, (length + 4) * plane)], orb, load_sem.at[1]
    )
    load_coef = pltpu.make_async_copy(coef_hbm, coef, load_sem.at[2])
    load_pot.start()
    load_orb.start()
    load_coef.start()

    matrix[...] = plane_matrix(doubled)
    source, target = iota((plane, 1), 0), iota((1, 2 * area), 1)
    inner = lax.rem(target, area)
    wanted = (lower + lax.div(inner, length)) * doubled + lower + lax.rem(inner, length)
    for k in range(2):
        select[k] = flag(source == jnp.where(lax.div(target, area) == k, wanted, -1), BF16)
    cells = length * area
    cell = iota((1, cells), 1)
    for f in range(6):
        inner = iota((area, 1), 0)
        major, minor = lax.div(inner, length), lax.rem(inner, length)
        layer = (length - 1) * (f % 2)
        picked_cell = (
            layer * area + inner, major * area + layer * length + minor, major * area + minor * length + layer
        )[f // 2]
        pick[pl.ds(f * area, area), :] = flag(cell == picked_cell, BF16)

    load_pot.wait()
    lanes = length * doubled
    flat = pot[...].reshape(area, length)
    spread = flag(lax.rem(iota((1, lanes), 1), doubled) == iota((length, 1), 0))
    keep = lax.div(iota((1, lanes), 1), doubled) == lax.rem(iota((area, 1), 0), length)
    spread_rows = jnp.where(keep, dot_full(flat, spread), 0.0)
    own = len(tile_slots)
    tiles[own] = jnp.sum(spread_rows.reshape(length, length, lanes), axis=1)
    top = jnp.max(jnp.max(pot[...], axis=0), axis=(0, 1), keepdims=True)
    max1[0] = jnp.broadcast_to(top, max1.shape[1:])

    pl.semaphore_wait(barrier, len(greeted))

    sends = []
    for d, offset in enumerate(first):
        sends.append(remote(max1.at[0], max1.at[d + 1], m1_send.at[d], m1_recv.at[d], offset))
        sends[-1].start()
    tile_copies = []
    for s, slot in enumerate(tile_slots):
        copy = remote(tiles.at[own], tiles.at[s], tile_send.at[s], tile_recv.at[s], tile_to[slot])
        copy.start()
        tile_copies.append(copy)
    m1_copies = list(sends)
    sends += tile_copies

    load_coef.wait()
    v_copies = {}
    shared = [f for f in range(6) if f % 2 == 0 or sizes[f // 2] > 2]
    for f in shared:
        v_copies[f] = remote(coef, v_in.at[f ^ 1], v_send.at[f], v_recv.at[f ^ 1], faces[f])
    for f in shared[:2]:
        v_copies[f].start()
    sends += v_copies.values()

    load_orb.wait()

    def w(i):
        return orb[:, pl.ds(pl.multiple_of(i * plane, plane), plane)]

    @pl.loop(0, length + 2, unroll=2)
    def _(i):
        u[i] = dot2(w(i + 1), matrix[...]) - 0.5 * (w(i) + w(i + 2))

    for copy in m1_copies:
        copy.wait_recv()
    max2[0] = functools.reduce(jnp.maximum, [max1[d] for d in range(sizes[0])])
    m2_copies = []
    for d, offset in enumerate(second):
        copy = remote(max2.at[0], max2.at[d + 1], m2_send.at[d], m2_recv.at[d], offset)
        copy.start()
        m2_copies.append(copy)
    sends += m2_copies

    for copy in tile_copies:
        copy.wait_recv()
    for a in range(2):
        for b in range(2):
            low, high = tiles[4 * a + 2 * b], tiles[4 * a + 2 * b + 1]
            wide[pl.ds(a * length, length), pl.ds(b * lanes, lanes)] = low + pltpu.roll(high, length, 1)

    def potential(x):
        return wide[pl.ds(x, 1), :]

    @pl.loop(0, length + 2)
    def _(i):
        u[i] = u[i] + potential(i + lower - 1) * w(i + 1)

    @pl.loop(0, length, unroll=2)
    def _(i):
        centre_plane = u[i + 1]
        v[i] = dot2(centre_plane, matrix[...]) + potential(i + lower) * centre_plane - 0.5 * (u[i] + u[i + 2])

    for copy in m2_copies:
        copy.wait_recv()
    for f in shared[2:]:
        v_copies[f].start()

    top = functools.reduce(jnp.maximum, [max2[d] for d in range(sizes[1] * sizes[2])])[0:1, 0:1] + 6.0
    centre = (top + CUTOFF) / 2.0
    width = (top - CUTOFF) / 2.0
    away = centre - SHIFT
    alpha = 2.0 / (width * width)
    beta = -2.0 * away * alpha
    gamma = away * away * alpha - 1.0

    def filtered(i):
        return alpha * v[i] + beta * u[i + 1] + gamma * w(i + 2)

    @pl.loop(0, length // 2)
    def _(pair):
        here = pl.ds(pl.multiple_of(pair * 2 * area, 2 * area), 2 * area)
        rest[:, here] = dot2(filtered(2 * pair), select[0]) + dot2(filtered(2 * pair + 1), select[1])

    r = rest[...]
    r_s = split(r)
    gram = dot3(r_s, r_s, NT)
    sigma = jnp.sqrt(jnp.sum(jnp.sum(gram * gram, axis=1, keepdims=True), axis=0, keepdims=True))
    eye = flag(iota((rows, rows), 0) == iota((rows, rows), 1))
    product = gram * (1.0 / sigma)

    def pick_face(f):
        here = pl.ds(pl.multiple_of(f * area, area), area)
        rest_faces[here, :] = dot(pick[here, :], r_s[0], NT) + dot(pick[here, :], r_s[1], NT)

    def newton(step, state):
        product, inverse = state
        factor = 1.5 * eye - 0.5 * product
        factor_s = split(factor)
        once = dot3(split(product), factor_s)
        inverse = dot3(split(inverse), factor_s)
        pick_face(step)
        return dot3(split(once), factor_s), inverse

    product, inverse = lax.fori_loop(0, NEWTON - 1, newton, (product, eye))
    for f in range(NEWTON - 1, 6):
        pick_face(f)
    inverse = dot3(split(inverse), split(1.5 * eye - 0.5 * product))
    root = inverse * lax.rsqrt(sigma)
    root_s = split(root)

    rest_faces_s = split(rest_faces[...])
    facet[...] = dot3(rest_faces_s, root_s, NT)
    f_copies = []
    face_copies = []
    for f, offset in enumerate(faces):
        if sizes[f // 2] > 2:
            face_copies.append((f, pl.ds(f * area, area), pl.ds((f ^ 1) * area, area), offset))
        elif f % 2 == 0:
            both = pl.ds(f * area, 2 * area)
            face_copies.append((f, both, both, offset))
    for f, here, there, offset in face_copies:
        copy = remote(facet.at[here, :], ft_in.at[there, :], f_send.at[f], f_recv.at[f], offset)
        copy.start()
        f_copies.append(copy)
    sends += f_copies

    facet_s = split(facet[...])
    inverse_width = 1.0 / width
    slots = []
    for f in range(6):
        slots.append(rest_faces[pl.ds((f if sizes[f // 2] > 2 else f ^ 1) * area, area), :])
    slots_s = split(jnp.concatenate(slots, axis=0))
    couple = split((-0.5 * inverse_width) * dot3(root_s, slots_s, NT))
    own_wide = dot2(wide[pl.ds(lower, length), :], select[0])
    own_odd = pltpu.roll(own_wide, area, 1)
    own_potential = jnp.concatenate(
        [own_wide[k : k + 1, :] + own_odd[k + 1 : k + 2, :] for k in range(0, length, 2)], axis=1
    )
    around = jnp.zeros_like(r)
    for stride in (area, length, 1):
        coordinate = lax.rem(lax.div(cell, stride), length)
        around = around + flag(coordinate > 0) * pltpu.roll(r, stride, 1)
        around = around + flag(coordinate < length - 1) * pltpu.roll(r, cells - stride, 1)
    boxed = (3.0 + own_potential) * r - 0.5 * around
    energy = dot3(split(boxed), r_s, NT)
    block = dot3(split(dot3(root_s, split(energy))), root_s, NT)
    diagonal = split(inverse_width * (block - centre * eye))

    prior = coef[...]
    current = dot3(diagonal, split(prior))
    for copy in v_copies.values():
        copy.wait_recv()
    came = [split(v_in[f if f ^ 1 in shared else f ^ 1]) for f in range(6)]
    carried = []
    for copy in f_copies:
        copy.wait_recv()
    for f in range(6):
        carried.append(dot3(split(ft_in[pl.ds(f * area, area), :]), came[f]))
    current = current + dot3(couple, split(jnp.concatenate(carried, axis=0)))

    def send_projected(number, part, vectors):
        p_out[number, part] = dot3(facet_s, split(vectors))
        copies = []
        for f, here, there, offset in face_copies:
            copy = remote(
                p_out.at[number, part, here, :], p_in.at[number, part, there, :],
                p_send.at[number, part, f], p_recv.at[number, part, f], offset,
            )
            copy.start()
            copies.append(copy)
        return copies

    prior = [prior[:, k * half : (k + 1) * half] for k in range(PARTS)]
    current = [current[:, k * half : (k + 1) * half] for k in range(PARTS)]
    flying = [send_projected(0, part, current[part]) for part in range(PARTS)]
    for number in range(2):
        following, next_flying = [], []
        for part in range(PARTS):
            mine = 2.0 * dot3(diagonal, split(current[part])) - prior[part]
            for copy in flying[part]:
                copy.wait_recv()
            sends += flying[part]
            mine = mine + 2.0 * dot3(couple, split(p_in[number, part]))
            following.append(mine)
            if number == 0:
                next_flying.append(send_projected(1, part, mine))
            else:
                out_ref[:, pl.ds(part * half, half)] = mine
        prior, current, flying = current, following, next_flying

    for copy in sends:
        copy.wait_send()


def per_device(sizes, orbitals, potential, coefficients):
    length = potential.shape[0]
    rows, cells = orbitals.shape[-2:]
    cols = coefficients.shape[-1]
    doubled, area = 2 * length, length * length
    plane, lanes = doubled * doubled, length * doubled
    others = sizes[1] * sizes[2]
    dma = pltpu.SemaphoreType.DMA
    result = pl.pallas_call(
        functools.partial(kernel, length, sizes),
        out_shape=jax.ShapeDtypeStruct((rows, cols), F32),
        in_specs=[pl.BlockSpec(memory_space=pltpu.HBM)] * 3,
        out_specs=pl.BlockSpec(memory_space=pltpu.VMEM),
        scratch_shapes=[
            pltpu.VMEM((plane, plane), BF16),
            pltpu.VMEM((2, plane, 2 * area), BF16),
            pltpu.VMEM((6 * area, length * area), BF16),
            pltpu.VMEM((rows, (length + 4) * plane), F32),
            pltpu.VMEM((length, length, length), F32),
            pltpu.VMEM((rows, cols), F32),
            pltpu.VMEM((8, length, lanes), F32),
            pltpu.VMEM((sizes[0], 8, 128), F32),
            pltpu.VMEM((others, 8, 128), F32),
            pltpu.VMEM((doubled, plane), F32),
            pltpu.VMEM((length + 2, rows, plane), F32),
            pltpu.VMEM((length, rows, plane), F32),
            pltpu.VMEM((rows, length * area), F32),
            pltpu.VMEM((6 * area, rows), F32),
            pltpu.VMEM((6 * area, rows), F32),
            pltpu.VMEM((6 * area, rows), F32),
            pltpu.VMEM((6, rows, cols), F32),
            pltpu.VMEM((2, PARTS, 6 * area, cols // PARTS), F32),
            pltpu.VMEM((2, PARTS, 6 * area, cols // PARTS), F32),
            dma((3,)),
            dma((7,)),
            dma((7,)),
            dma((max(sizes[0] - 1, 1),)),
            dma((max(sizes[0] - 1, 1),)),
            dma((max(others - 1, 1),)),
            dma((max(others - 1, 1),)),
            dma((6,)),
            dma((6,)),
            dma((6,)),
            dma((6,)),
            dma((2, PARTS, 6)),
            dma((2, PARTS, 6)),
        ],
        compiler_params=pltpu.CompilerParams(
            collective_id=0, has_side_effects=True, vmem_limit_bytes=60 * 1024 * 1024
        ),
    )(orbitals.reshape(rows, cells), potential, coefficients.reshape(rows, cols))
    return result.reshape(coefficients.shape)


def solution(mesh):
    sizes = tuple(mesh.shape[a] for a in AXES)
    placed = (P("gx", "gy", "gz", None, None), P("gx", "gy", "gz"), P("gx", "gy", "gz", None, None))
    return jax.shard_map(
        functools.partial(per_device, sizes),
        mesh=mesh,
        in_specs=placed,
        out_specs=P("gx", "gy", "gz", None, None),
        check_vma=False,
    )
```

```python
import functools
import itertools

import jax
import jax.numpy as jnp
from jax import lax
from jax.experimental import pallas as pl
from jax.experimental.pallas import tpu as pltpu
from jax.sharding import PartitionSpec as P

NEWTON = 6
PARTS = 2
CUTOFF = 1.0
SHIFT = 4.0
AXES = ("gx", "gy", "gz")
MESH = pl.DeviceIdType.MESH
F32 = jnp.float32
BF16 = jnp.bfloat16
NT = (((1,), (1,)), ((), ()))
NN = (((1,), (0,)), ((), ()))


def iota(shape, dim):
    return lax.broadcasted_iota(jnp.int32, shape, dim)


def split(a):
    high = a.astype(BF16)
    return high, (a - high.astype(F32)).astype(BF16)


def dot(a, b, dims=NN):
    return lax.dot_general(a, b, dims, preferred_element_type=F32)


def dot_full(a, b, dims=NN):
    return lax.dot_general(a, b, dims, precision=lax.Precision.HIGHEST, preferred_element_type=F32)


def dot3(a, b, dims=NN):
    rows = a[0].shape[0]
    both = dot(jnp.concatenate(a, axis=0), b[0], dims)
    return both[:rows] + (both[rows:] + dot(a[0], b[1], dims))


def dot2(a, b, dims=NN):
    rows = a.shape[0]
    both = dot(jnp.concatenate(split(a), axis=0), b, dims)
    return both[:rows] + both[rows:]


def dot2r(a, b, dims=NN):
    high, low = split(b)
    return dot(a, high, dims) + dot(a, low, dims)


def flag(condition, dtype=F32):
    return jnp.where(condition, 1.0, 0.0).astype(dtype)


def plane_matrix(width):
    cells = width * width
    row, col = iota((cells, 1), 0), iota((1, cells), 1)
    gap = row - col
    inside = lax.div(row, width) == lax.div(col, width)
    near = ((jnp.abs(gap) == 1) & inside) | (jnp.abs(gap) == width)
    return (jnp.where(gap == 0, 3.0 - SHIFT, 0.0) - 0.5 * flag(near)).astype(BF16)


def max_stages(sizes):
    reach = [range(0, n, 2) for n in sizes]
    every = [o for o in itertools.product(*reach) if any(o)]
    if len(every) < 8:
        return [every]
    stages = []
    for axis in range(3):
        if len(reach[axis]) > 1:
            stages.append([tuple(d if k == axis else 0 for k in range(3)) for d in reach[axis][1:]])
    return stages


def kernel(
    length, sizes, orb_hbm, pot_hbm, coef_hbm, out_ref,
    matrix, select, pick, orb, pot, coef, tiles, tops, tops_in, wide, u, v, own_w, own_u, own_v, rest_faces, facet, ft_in, v_in, p_out, p_in,
    load_sem, tile_send, tile_recv, top_send, top_recv,
    v_send, v_recv, f_send, f_recv, p_send, p_recv,
):
    me = [lax.axis_index(a) for a in AXES]
    rows, cols = coef.shape
    doubled, area = 2 * length, length * length
    plane, lower = doubled * doubled, length // 2
    half = cols // PARTS

    def at(offset):
        return tuple(lax.rem(me[k] + (offset[k] % sizes[k]), sizes[k]) for k in range(3))

    def remote(src, dst, send, recv, offset):
        return pltpu.make_async_remote_copy(
            src_ref=src, dst_ref=dst, send_sem=send, recv_sem=recv, device_id=at(offset), device_id_type=MESH
        )

    tile_slots = [s for s in itertools.product((0, 1), repeat=3) if s != (1, 1, 1)]
    tile_to = {s: tuple(1 - k for k in s) for s in tile_slots}
    stages = max_stages(sizes)
    faces = []
    for axis in range(3):
        for side in (-1, 1):
            faces.append(tuple(side if k == axis else 0 for k in range(3)))

    def wrapped(offset):
        return tuple(o % n for o, n in zip(offset, sizes))

    greeted = set()
    for offset in list(tile_to.values()) + sum(stages, []) + faces:
        greeted.add(wrapped(offset))
        greeted.add(wrapped(tuple(-o for o in offset)))
    greeted = sorted(greeted)

    barrier = pltpu.get_barrier_semaphore()
    for offset in greeted:
        pl.semaphore_signal(barrier, inc=1, device_id=at(offset), device_id_type=MESH)

    load_pot = pltpu.make_async_copy(pot_hbm, pot, load_sem.at[0])
    load_orb = pltpu.make_async_copy(
        orb_hbm.at[:, pl.ds((lower - 2) * plane, (length + 4) * plane)], orb, load_sem.at[1]
    )
    load_coef = pltpu.make_async_copy(coef_hbm, coef, load_sem.at[2])
    load_pot.start()
    load_orb.start()
    load_coef.start()

    matrix[...] = plane_matrix(doubled)
    source, target = iota((plane, 1), 0), iota((1, 2 * area), 1)
    inner = lax.rem(target, area)
    wanted = (lower + lax.div(inner, length)) * doubled + lower + lax.rem(inner, length)
    for k in range(2):
        select[k] = flag(source == jnp.where(lax.div(target, area) == k, wanted, -1), BF16)
    cells = length * area
    cell = iota((1, cells), 1)
    for f in range(6):
        inner = iota((area, 1), 0)
        major, minor = lax.div(inner, length), lax.rem(inner, length)
        layer = (length - 1) * (f % 2)
        picked_cell = (
            layer * area + inner, major * area + layer * length + minor, major * area + minor * length + layer
        )[f // 2]
        pick[pl.ds(f * area, area), :] = flag(cell == picked_cell, BF16)

    load_pot.wait()
    lanes = length * doubled
    flat = pot[...].reshape(area, length)
    spread = flag(lax.rem(iota((1, lanes), 1), doubled) == iota((length, 1), 0))
    keep = lax.div(iota((1, lanes), 1), doubled) == lax.rem(iota((area, 1), 0), length)
    spread_rows = jnp.where(keep, dot_full(flat, spread), 0.0)
    own = len(tile_slots)
    tiles[own] = jnp.sum(spread_rows.reshape(length, length, lanes), axis=1)

    pl.semaphore_wait(barrier, len(greeted))

    sends = []
    tile_copies = []
    for s, slot in enumerate(tile_slots):
        copy = remote(tiles.at[own], tiles.at[s], tile_send.at[s], tile_recv.at[s], tile_to[slot])
        copy.start()
        tile_copies.append(copy)
    sends += tile_copies

    load_coef.wait()
    v_copies = {}
    shared = [f for f in range(6) if f % 2 == 0 or sizes[f // 2] > 2]
    for f in shared:
        v_copies[f] = remote(coef, v_in.at[f ^ 1], v_send.at[f], v_recv.at[f ^ 1], faces[f])
    for f in shared[:2]:
        v_copies[f].start()
    sends += v_copies.values()

    load_orb.wait()

    def w(i):
        return orb[:, pl.ds(pl.multiple_of(i * plane, plane), plane)]

    def pair_lanes(pair):
        return pl.ds(pl.multiple_of(pair * 2 * area, 2 * area), 2 * area)

    def own_cells(even, odd):
        return dot2(even, select[0]) + dot2(odd, select[1])

    @pl.loop(0, length + 2, unroll=2)
    def _(i):
        u[i] = dot2(w(i + 1), matrix[...]) - 0.5 * (w(i) + w(i + 2))

    @pl.loop(0, length // 2)
    def _(pair):
        own_w[:, pair_lanes(pair)] = own_cells(w(2 * pair + 2), w(2 * pair + 3))

    for copy in tile_copies:
        copy.wait_recv()
    for a in range(2):
        for b in range(2):
            low, high = tiles[4 * a + 2 * b], tiles[4 * a + 2 * b + 1]
            wide[pl.ds(a * length, length), pl.ds(b * lanes, lanes)] = low + pltpu.roll(high, length, 1)

    sent = 0
    flying = []

    def send_max(stage):
        copies = []
        for d, offset in enumerate(stages[stage]):
            k = sent + d
            copy = remote(
                tops.at[stage], tops_in.at[k], top_send.at[k], top_recv.at[k], offset
            )
            copy.start()
            copies.append(copy)
        return copies

    def gather_max(stage, copies):
        for copy in copies:
            copy.wait_recv()
        return functools.reduce(
            jnp.maximum, [tops_in[sent + d] for d in range(len(stages[stage]))], tops[stage]
        )

    top = jnp.max(jnp.max(wide[...], axis=1, keepdims=True), axis=0, keepdims=True)
    tops[0] = jnp.broadcast_to(top, tops.shape[1:])
    flying = send_max(0)
    sends += flying

    def potential(x):
        return wide[pl.ds(x, 1), :]

    @pl.loop(0, length + 2)
    def _(i):
        u[i] = u[i] + potential(i + lower - 1) * w(i + 1)

    @pl.loop(0, length, unroll=2)
    def _(i):
        centre_plane = u[i + 1]
        v[i] = dot2(centre_plane, matrix[...]) + potential(i + lower) * centre_plane - 0.5 * (u[i] + u[i + 2])

    @pl.loop(0, length // 2)
    def _(pair):
        own_u[:, pair_lanes(pair)] = own_cells(u[2 * pair + 1], u[2 * pair + 2])
        own_v[:, pair_lanes(pair)] = own_cells(v[2 * pair], v[2 * pair + 1])

    for stage in range(1, len(stages)):
        tops[stage] = gather_max(stage - 1, flying)
        sent += len(stages[stage - 1])
        flying = send_max(stage)
        sends += flying
    top = gather_max(len(stages) - 1, flying)
    for f in shared[2:]:
        v_copies[f].start()

    top = top[0:1, 0:1] + 6.0
    centre = (top + CUTOFF) / 2.0
    width = (top - CUTOFF) / 2.0
    away = centre - SHIFT
    alpha = 2.0 / (width * width)
    beta = -2.0 * away * alpha
    gamma = away * away * alpha - 1.0

    r = alpha * own_v[...] + beta * own_u[...] + gamma * own_w[...]
    r_s = split(r)
    gram = dot3(r_s, r_s, NT)
    sigma = jnp.sqrt(jnp.sum(jnp.sum(gram * gram, axis=1, keepdims=True), axis=0, keepdims=True))
    eye = flag(iota((rows, rows), 0) == iota((rows, rows), 1))
    product = gram * (1.0 / sigma)

    def pick_face(f):
        here = pl.ds(pl.multiple_of(f * area, area), area)
        rest_faces[here, :] = dot(pick[here, :], r_s[0], NT) + dot(pick[here, :], r_s[1], NT)

    def newton(step, state):
        product, inverse = state
        factor = 1.5 * eye - 0.5 * product
        factor_s = split(factor)
        once = dot3(split(product), factor_s)
        inverse = dot3(split(inverse), factor_s)
        pick_face(step)
        return dot3(split(once), factor_s), inverse

    product, inverse = lax.fori_loop(0, NEWTON - 1, newton, (product, eye))
    for f in range(NEWTON - 1, 6):
        pick_face(f)
    inverse = dot3(split(inverse), split(1.5 * eye - 0.5 * product))
    root = inverse * lax.rsqrt(sigma)
    root_s = split(root)

    rest_faces_s = split(rest_faces[...])
    facet[...] = dot3(rest_faces_s, root_s, NT)
    f_copies = []
    face_copies = []
    for f, offset in enumerate(faces):
        if sizes[f // 2] > 2:
            face_copies.append((f, pl.ds(f * area, area), pl.ds((f ^ 1) * area, area), offset))
        elif f % 2 == 0:
            both = pl.ds(f * area, 2 * area)
            face_copies.append((f, both, both, offset))
    for f, here, there, offset in face_copies:
        copy = remote(facet.at[here, :], ft_in.at[there, :], f_send.at[f], f_recv.at[f], offset)
        copy.start()
        f_copies.append(copy)
    sends += f_copies

    facet_s = split(facet[...])
    inverse_width = 1.0 / width
    slots = []
    for f in range(6):
        slots.append(rest_faces[pl.ds((f if sizes[f // 2] > 2 else f ^ 1) * area, area), :])
    slots_s = split(jnp.concatenate(slots, axis=0))
    couple = split((-0.5 * inverse_width) * dot3(root_s, slots_s, NT))
    own_wide = dot2(wide[pl.ds(lower, length), :], select[0])
    own_odd = pltpu.roll(own_wide, area, 1)
    own_potential = jnp.concatenate(
        [own_wide[k : k + 1, :] + own_odd[k + 1 : k + 2, :] for k in range(0, length, 2)], axis=1
    )
    around = jnp.zeros_like(r)
    for stride in (area, length, 1):
        coordinate = lax.rem(lax.div(cell, stride), length)
        around = around + flag(coordinate > 0) * pltpu.roll(r, stride, 1)
        around = around + flag(coordinate < length - 1) * pltpu.roll(r, cells - stride, 1)
    boxed = (3.0 + own_potential) * r - 0.5 * around
    energy = dot3(split(boxed), r_s, NT)
    block = dot3(split(dot3(root_s, split(energy))), root_s, NT)
    diagonal = split(inverse_width * (block - centre * eye))

    prior = coef[...]
    current = dot3(diagonal, split(prior))
    for copy in v_copies.values():
        copy.wait_recv()
    came = [split(v_in[f if f ^ 1 in shared else f ^ 1]) for f in range(6)]
    carried = []
    for copy in f_copies:
        copy.wait_recv()
    for f in range(6):
        carried.append(dot3(split(ft_in[pl.ds(f * area, area), :]), came[f]))
    current = current + dot3(couple, split(jnp.concatenate(carried, axis=0)))

    def send_projected(number, part, vectors):
        p_out[number, part] = dot3(facet_s, split(vectors))
        copies = []
        for f, here, there, offset in face_copies:
            copy = remote(
                p_out.at[number, part, here, :], p_in.at[number, part, there, :],
                p_send.at[number, part, f], p_recv.at[number, part, f], offset,
            )
            copy.start()
            copies.append(copy)
        return copies

    prior = [prior[:, k * half : (k + 1) * half] for k in range(PARTS)]
    current = [current[:, k * half : (k + 1) * half] for k in range(PARTS)]
    flying = [send_projected(0, part, current[part]) for part in range(PARTS)]
    for number in range(2):
        following, next_flying = [], []
        for part in range(PARTS):
            mine = 2.0 * dot3(diagonal, split(current[part])) - prior[part]
            for copy in flying[part]:
                copy.wait_recv()
            sends += flying[part]
            mine = mine + 2.0 * dot3(couple, split(p_in[number, part]))
            following.append(mine)
            if number == 0:
                next_flying.append(send_projected(1, part, mine))
            else:
                out_ref[:, pl.ds(part * half, half)] = mine
        prior, current, flying = current, following, next_flying

    for copy in sends:
        copy.wait_send()


def per_device(sizes, orbitals, potential, coefficients):
    length = potential.shape[0]
    rows, cells = orbitals.shape[-2:]
    cols = coefficients.shape[-1]
    doubled, area = 2 * length, length * length
    plane, lanes = doubled * doubled, length * doubled
    stages = max_stages(sizes)
    top_copies = max(sum(len(stage) for stage in stages), 1)
    dma = pltpu.SemaphoreType.DMA
    result = pl.pallas_call(
        functools.partial(kernel, length, sizes),
        out_shape=jax.ShapeDtypeStruct((rows, cols), F32),
        in_specs=[pl.BlockSpec(memory_space=pltpu.HBM)] * 3,
        out_specs=pl.BlockSpec(memory_space=pltpu.VMEM),
        scratch_shapes=[
            pltpu.VMEM((plane, plane), BF16),
            pltpu.VMEM((2, plane, 2 * area), BF16),
            pltpu.VMEM((6 * area, length * area), BF16),
            pltpu.VMEM((rows, (length + 4) * plane), F32),
            pltpu.VMEM((length, length, length), F32),
            pltpu.VMEM((rows, cols), F32),
            pltpu.VMEM((8, length, lanes), F32),
            pltpu.VMEM((len(stages), 8, 128), F32),
            pltpu.VMEM((top_copies, 8, 128), F32),
            pltpu.VMEM((doubled, plane), F32),
            pltpu.VMEM((length + 2, rows, plane), F32),
            pltpu.VMEM((length, rows, plane), F32),
            pltpu.VMEM((rows, length * area), F32),
            pltpu.VMEM((rows, length * area), F32),
            pltpu.VMEM((rows, length * area), F32),
            pltpu.VMEM((6 * area, rows), F32),
            pltpu.VMEM((6 * area, rows), F32),
            pltpu.VMEM((6 * area, rows), F32),
            pltpu.VMEM((6, rows, cols), F32),
            pltpu.VMEM((2, PARTS, 6 * area, cols // PARTS), F32),
            pltpu.VMEM((2, PARTS, 6 * area, cols // PARTS), F32),
            dma((3,)),
            dma((7,)),
            dma((7,)),
            dma((top_copies,)),
            dma((top_copies,)),
            dma((6,)),
            dma((6,)),
            dma((6,)),
            dma((6,)),
            dma((2, PARTS, 6)),
            dma((2, PARTS, 6)),
        ],
        compiler_params=pltpu.CompilerParams(
            collective_id=0, has_side_effects=True, vmem_limit_bytes=60 * 1024 * 1024
        ),
    )(orbitals.reshape(rows, cells), potential, coefficients.reshape(rows, cols))
    return result.reshape(coefficients.shape)


def solution(mesh):
    sizes = tuple(mesh.shape[a] for a in AXES)
    placed = (P("gx", "gy", "gz", None, None), P("gx", "gy", "gz"), P("gx", "gy", "gz", None, None))
    return jax.shard_map(
        functools.partial(per_device, sizes),
        mesh=mesh,
        in_specs=placed,
        out_specs=P("gx", "gy", "gz", None, None),
        check_vma=False,
    )
```

```python
import functools
import itertools

import jax
import jax.numpy as jnp
from jax import lax
from jax.experimental import pallas as pl
from jax.experimental.pallas import tpu as pltpu
from jax.sharding import PartitionSpec as P

NEWTON = 6
PARTS = 2
CUTOFF = 1.0
SHIFT = 4.0
AXES = ("gx", "gy", "gz")
MESH = pl.DeviceIdType.MESH
F32 = jnp.float32
BF16 = jnp.bfloat16
NT = (((1,), (1,)), ((), ()))
NN = (((1,), (0,)), ((), ()))


def iota(shape, dim):
    return lax.broadcasted_iota(jnp.int32, shape, dim)


def split(a):
    high = a.astype(BF16)
    return high, (a - high.astype(F32)).astype(BF16)


def dot(a, b, dims=NN):
    return lax.dot_general(a, b, dims, preferred_element_type=F32)


def dot_full(a, b, dims=NN):
    return lax.dot_general(a, b, dims, precision=lax.Precision.HIGHEST, preferred_element_type=F32)


def dot3(a, b, dims=NN):
    rows = a[0].shape[0]
    both = dot(jnp.concatenate(a, axis=0), b[0], dims)
    return both[:rows] + (both[rows:] + dot(a[0], b[1], dims))


def dot2(a, b, dims=NN):
    rows = a.shape[0]
    both = dot(jnp.concatenate(split(a), axis=0), b, dims)
    return both[:rows] + both[rows:]


def dot2r(a, b, dims=NN):
    high, low = split(b)
    return dot(a, high, dims) + dot(a, low, dims)


def flag(condition, dtype=F32):
    return jnp.where(condition, 1.0, 0.0).astype(dtype)


def plane_matrix(width):
    cells = width * width
    row, col = iota((cells, 1), 0), iota((1, cells), 1)
    gap = row - col
    inside = lax.div(row, width) == lax.div(col, width)
    near = ((jnp.abs(gap) == 1) & inside) | (jnp.abs(gap) == width)
    return (jnp.where(gap == 0, 3.0 - SHIFT, 0.0) - 0.5 * flag(near)).astype(BF16)


def max_stages(sizes):
    reach = [range(0, n, 2) for n in sizes]
    every = [o for o in itertools.product(*reach) if any(o)]
    if len(every) < 8:
        return [every]
    stages = []
    for axis in range(3):
        if len(reach[axis]) > 1:
            stages.append([tuple(d if k == axis else 0 for k in range(3)) for d in reach[axis][1:]])
    return stages


def kernel(
    length, sizes, orb_hbm, pot_hbm, coef_hbm, out_ref,
    matrix, select, pick, orb, pot, coef, tiles, tops, tops_in, wide, u, v, own_w, own_u, own_v, rest_faces, facet, ft_in, v_in, p_out, p_in,
    load_sem, tile_send, tile_recv, top_send, top_recv,
    v_send, v_recv, f_send, f_recv, p_send, p_recv,
):
    me = [lax.axis_index(a) for a in AXES]
    rows, cols = coef.shape
    doubled, area = 2 * length, length * length
    plane, lower = doubled * doubled, length // 2
    half = cols // PARTS

    moved = [[me[k]] + [lax.rem(me[k] + d, sizes[k]) for d in range(1, sizes[k])] for k in range(3)]

    def at(offset):
        return tuple(moved[k][offset[k] % sizes[k]] for k in range(3))

    def finish(region, sem):
        pltpu.make_async_copy(region, region, sem).wait()

    def remote(src, dst, send, recv, offset):
        return pltpu.make_async_remote_copy(
            src_ref=src, dst_ref=dst, send_sem=send, recv_sem=recv, device_id=at(offset), device_id_type=MESH
        )

    tile_slots = [s for s in itertools.product((0, 1), repeat=3) if s != (1, 1, 1)]
    tile_to = {s: tuple(1 - k for k in s) for s in tile_slots}
    stages = max_stages(sizes)
    faces = []
    for axis in range(3):
        for side in (-1, 1):
            faces.append(tuple(side if k == axis else 0 for k in range(3)))

    def wrapped(offset):
        return tuple(o % n for o, n in zip(offset, sizes))

    greeted = set()
    for offset in list(tile_to.values()) + sum(stages, []) + faces:
        greeted.add(wrapped(offset))
        greeted.add(wrapped(tuple(-o for o in offset)))
    greeted = sorted(greeted)

    barrier = pltpu.get_barrier_semaphore()
    for offset in greeted:
        pl.semaphore_signal(barrier, inc=1, device_id=at(offset), device_id_type=MESH)

    load_pot = pltpu.make_async_copy(pot_hbm, pot, load_sem.at[0])
    load_orb = pltpu.make_async_copy(
        orb_hbm.at[:, pl.ds((lower - 2) * plane, (length + 4) * plane)], orb, load_sem.at[1]
    )
    load_coef = pltpu.make_async_copy(coef_hbm, coef, load_sem.at[2])
    load_pot.start()
    load_orb.start()
    load_coef.start()

    matrix[...] = plane_matrix(doubled)
    source, target = iota((plane, 1), 0), iota((1, 2 * area), 1)
    inner = lax.rem(target, area)
    wanted = (lower + lax.div(inner, length)) * doubled + lower + lax.rem(inner, length)
    for k in range(2):
        select[k] = flag(source == jnp.where(lax.div(target, area) == k, wanted, -1), BF16)
    cells = length * area
    cell = iota((1, cells), 1)
    for f in range(6):
        inner = iota((area, 1), 0)
        major, minor = lax.div(inner, length), lax.rem(inner, length)
        layer = (length - 1) * (f % 2)
        picked_cell = (
            layer * area + inner, major * area + layer * length + minor, major * area + minor * length + layer
        )[f // 2]
        pick[pl.ds(f * area, area), :] = flag(cell == picked_cell, BF16)

    load_pot.wait()
    lanes = length * doubled
    flat = pot[...].reshape(area, length)
    spread = flag(lax.rem(iota((1, lanes), 1), doubled) == iota((length, 1), 0))
    keep = lax.div(iota((1, lanes), 1), doubled) == lax.rem(iota((area, 1), 0), length)
    spread_rows = jnp.where(keep, dot_full(flat, spread), 0.0)
    own = len(tile_slots)
    tiles[own] = jnp.sum(spread_rows.reshape(length, length, lanes), axis=1)

    pl.semaphore_wait(barrier, len(greeted))

    for s, slot in enumerate(tile_slots):
        copy = remote(tiles.at[own], tiles.at[s], tile_send, tile_recv, tile_to[slot])
        copy.start()

    load_coef.wait()
    v_copies = {}
    shared = [f for f in range(6) if f % 2 == 0 or sizes[f // 2] > 2]
    for k, f in enumerate(shared):
        v_copies[f] = remote(coef, v_in.at[k], v_send, v_recv, faces[f])
    for f in shared[:2]:
        v_copies[f].start()

    load_orb.wait()

    def w(i):
        return orb[:, pl.ds(pl.multiple_of(i * plane, plane), plane)]

    def pair_lanes(pair):
        return pl.ds(pl.multiple_of(pair * 2 * area, 2 * area), 2 * area)

    def own_cells(even, odd):
        return dot2(even, select[0]) + dot2(odd, select[1])

    @pl.loop(0, length + 2, unroll=2)
    def _(i):
        u[i] = dot2(w(i + 1), matrix[...]) - 0.5 * (w(i) + w(i + 2))

    @pl.loop(0, length // 2)
    def _(pair):
        own_w[:, pair_lanes(pair)] = own_cells(w(2 * pair + 2), w(2 * pair + 3))

    finish(tiles.at[pl.ds(0, own)], tile_recv)
    for a in range(2):
        for b in range(2):
            low, high = tiles[4 * a + 2 * b], tiles[4 * a + 2 * b + 1]
            wide[pl.ds(a * length, length), pl.ds(b * lanes, lanes)] = low + pltpu.roll(high, length, 1)

    sent = 0

    def send_max(stage):
        for d, offset in enumerate(stages[stage]):
            k = sent + d
            copy = remote(
                tops.at[stage], tops_in.at[k], top_send.at[stage], top_recv.at[stage], offset
            )
            copy.start()

    def gather_max(stage):
        finish(tops_in.at[pl.ds(sent, len(stages[stage]))], top_recv.at[stage])
        return functools.reduce(
            jnp.maximum, [tops_in[sent + d] for d in range(len(stages[stage]))], tops[stage]
        )

    top = jnp.max(jnp.max(wide[...], axis=1, keepdims=True), axis=0, keepdims=True)
    tops[0] = jnp.broadcast_to(top, tops.shape[1:])
    send_max(0)

    def potential(x):
        return wide[pl.ds(x, 1), :]

    @pl.loop(0, length + 2)
    def _(i):
        u[i] = u[i] + potential(i + lower - 1) * w(i + 1)

    @pl.loop(0, length, unroll=2)
    def _(i):
        centre_plane = u[i + 1]
        v[i] = dot2(centre_plane, matrix[...]) + potential(i + lower) * centre_plane - 0.5 * (u[i] + u[i + 2])

    @pl.loop(0, length // 2)
    def _(pair):
        own_u[:, pair_lanes(pair)] = own_cells(u[2 * pair + 1], u[2 * pair + 2])
        own_v[:, pair_lanes(pair)] = own_cells(v[2 * pair], v[2 * pair + 1])

    for stage in range(1, len(stages)):
        tops[stage] = gather_max(stage - 1)
        sent += len(stages[stage - 1])
        send_max(stage)
    top = gather_max(len(stages) - 1)
    for f in shared[2:]:
        v_copies[f].start()

    top = top[0:1, 0:1] + 6.0
    centre = (top + CUTOFF) / 2.0
    width = (top - CUTOFF) / 2.0
    away = centre - SHIFT
    alpha = 2.0 / (width * width)
    beta = -2.0 * away * alpha
    gamma = away * away * alpha - 1.0

    r = alpha * own_v[...] + beta * own_u[...] + gamma * own_w[...]
    r_s = split(r)
    gram = dot3(r_s, r_s, NT)
    sigma = jnp.sqrt(jnp.sum(jnp.sum(gram * gram, axis=1, keepdims=True), axis=0, keepdims=True))
    eye = flag(iota((rows, rows), 0) == iota((rows, rows), 1))
    product = gram * (1.0 / sigma)

    def pick_face(f):
        here = pl.ds(pl.multiple_of(f * area, area), area)
        rest_faces[here, :] = dot(pick[here, :], r_s[0], NT) + dot(pick[here, :], r_s[1], NT)

    def newton(step, state):
        product, inverse = state
        factor = 1.5 * eye - 0.5 * product
        factor_s = split(factor)
        once = dot3(split(product), factor_s)
        inverse = dot3(split(inverse), factor_s)
        pick_face(step)
        return dot3(split(once), factor_s), inverse

    product, inverse = lax.fori_loop(0, NEWTON - 1, newton, (product, eye))
    for f in range(NEWTON - 1, 6):
        pick_face(f)
    inverse = dot3(split(inverse), split(1.5 * eye - 0.5 * product))
    root = inverse * lax.rsqrt(sigma)
    root_s = split(root)

    rest_faces_s = split(rest_faces[...])
    facet[...] = dot3(rest_faces_s, root_s, NT)
    face_copies = []
    for f, offset in enumerate(faces):
        if sizes[f // 2] > 2:
            face_copies.append((f, pl.ds(f * area, area), pl.ds((f ^ 1) * area, area), offset))
        elif f % 2 == 0:
            both = pl.ds(f * area, 2 * area)
            face_copies.append((f, both, both, offset))
    for f, here, there, offset in face_copies:
        copy = remote(facet.at[here, :], ft_in.at[there, :], f_send, f_recv, offset)
        copy.start()

    facet_s = split(facet[...])
    inverse_width = 1.0 / width
    slots = []
    for f in range(6):
        slots.append(rest_faces[pl.ds((f if sizes[f // 2] > 2 else f ^ 1) * area, area), :])
    slots_s = split(jnp.concatenate(slots, axis=0))
    couple = split((-0.5 * inverse_width) * dot3(root_s, slots_s, NT))
    own_wide = dot2(wide[pl.ds(lower, length), :], select[0])
    own_odd = pltpu.roll(own_wide, area, 1)
    own_potential = jnp.concatenate(
        [own_wide[k : k + 1, :] + own_odd[k + 1 : k + 2, :] for k in range(0, length, 2)], axis=1
    )
    around = jnp.zeros_like(r)
    for stride in (area, length, 1):
        coordinate = lax.rem(lax.div(cell, stride), length)
        around = around + flag(coordinate > 0) * pltpu.roll(r, stride, 1)
        around = around + flag(coordinate < length - 1) * pltpu.roll(r, cells - stride, 1)
    boxed = (3.0 + own_potential) * r - 0.5 * around
    energy = dot3(split(boxed), r_s, NT)
    block = dot3(split(dot3(root_s, split(energy))), root_s, NT)
    diagonal = split(inverse_width * (block - centre * eye))

    prior = coef[...]
    current = dot3(diagonal, split(prior))
    finish(tiles.at[pl.ds(0, own)], tile_send)
    for stage in range(len(stages)):
        finish(tops_in.at[pl.ds(0, len(stages[stage]))], top_send.at[stage])
    finish(v_in.at[pl.ds(0, len(shared))], v_send)
    finish(v_in.at[pl.ds(0, len(shared))], v_recv)
    came = [split(v_in[shared.index(f ^ 1 if f ^ 1 in shared else f)]) for f in range(6)]
    carried = []
    finish(ft_in, f_recv)
    for f in range(6):
        carried.append(dot3(split(ft_in[pl.ds(f * area, area), :]), came[f]))
    current = current + dot3(couple, split(jnp.concatenate(carried, axis=0)))

    def send_projected(number, part, vectors):
        p_out[number, part] = dot3(facet_s, split(vectors))
        for f, here, there, offset in face_copies:
            copy = remote(
                p_out.at[number, part, here, :], p_in.at[number, part, there, :],
                p_send.at[number, part], p_recv.at[number, part], offset,
            )
            copy.start()

    prior = [prior[:, k * half : (k + 1) * half] for k in range(PARTS)]
    current = [current[:, k * half : (k + 1) * half] for k in range(PARTS)]
    for part in range(PARTS):
        send_projected(0, part, current[part])
    finish(facet, f_send)
    for number in range(2):
        following = []
        for part in range(PARTS):
            mine = 2.0 * dot3(diagonal, split(current[part])) - prior[part]
            if number == 1:
                finish(p_out.at[0, part], p_send.at[0, part])
            finish(p_in.at[number, part], p_recv.at[number, part])
            mine = mine + 2.0 * dot3(couple, split(p_in[number, part]))
            following.append(mine)
            if number == 0:
                send_projected(1, part, mine)
            else:
                out_ref[:, pl.ds(part * half, half)] = mine
        prior, current = current, following

    for part in range(PARTS):
        finish(p_out.at[1, part], p_send.at[1, part])


def per_device(sizes, orbitals, potential, coefficients):
    length = potential.shape[0]
    rows, cells = orbitals.shape[-2:]
    cols = coefficients.shape[-1]
    doubled, area = 2 * length, length * length
    plane, lanes = doubled * doubled, length * doubled
    stages = max_stages(sizes)
    top_copies = max(sum(len(stage) for stage in stages), 1)
    dma = pltpu.SemaphoreType.DMA
    result = pl.pallas_call(
        functools.partial(kernel, length, sizes),
        out_shape=jax.ShapeDtypeStruct((rows, cols), F32),
        in_specs=[pl.BlockSpec(memory_space=pltpu.HBM)] * 3,
        out_specs=pl.BlockSpec(memory_space=pltpu.VMEM),
        scratch_shapes=[
            pltpu.VMEM((plane, plane), BF16),
            pltpu.VMEM((2, plane, 2 * area), BF16),
            pltpu.VMEM((6 * area, length * area), BF16),
            pltpu.VMEM((rows, (length + 4) * plane), F32),
            pltpu.VMEM((length, length, length), F32),
            pltpu.VMEM((rows, cols), F32),
            pltpu.VMEM((8, length, lanes), F32),
            pltpu.VMEM((len(stages), 8, 128), F32),
            pltpu.VMEM((top_copies, 8, 128), F32),
            pltpu.VMEM((doubled, plane), F32),
            pltpu.VMEM((length + 2, rows, plane), F32),
            pltpu.VMEM((length, rows, plane), F32),
            pltpu.VMEM((rows, length * area), F32),
            pltpu.VMEM((rows, length * area), F32),
            pltpu.VMEM((rows, length * area), F32),
            pltpu.VMEM((6 * area, rows), F32),
            pltpu.VMEM((6 * area, rows), F32),
            pltpu.VMEM((6 * area, rows), F32),
            pltpu.VMEM((6, rows, cols), F32),
            pltpu.VMEM((2, PARTS, 6 * area, cols // PARTS), F32),
            pltpu.VMEM((2, PARTS, 6 * area, cols // PARTS), F32),
            dma((3,)),
            dma,
            dma,
            dma((max(len(stages), 1),)),
            dma((max(len(stages), 1),)),
            dma,
            dma,
            dma,
            dma,
            dma((2, PARTS)),
            dma((2, PARTS)),
        ],
        compiler_params=pltpu.CompilerParams(
            collective_id=0, has_side_effects=True, vmem_limit_bytes=60 * 1024 * 1024
        ),
    )(orbitals.reshape(rows, cells), potential, coefficients.reshape(rows, cols))
    return result.reshape(coefficients.shape)


def solution(mesh):
    sizes = tuple(mesh.shape[a] for a in AXES)
    placed = (P("gx", "gy", "gz", None, None), P("gx", "gy", "gz"), P("gx", "gy", "gz", None, None))
    return jax.shard_map(
        functools.partial(per_device, sizes),
        mesh=mesh,
        in_specs=placed,
        out_specs=P("gx", "gy", "gz", None, None),
        check_vma=False,
    )
```

```python
import functools
import itertools

import jax
import jax.numpy as jnp
from jax import lax
from jax.experimental import pallas as pl
from jax.experimental.pallas import tpu as pltpu
from jax.sharding import PartitionSpec as P

NEWTON = 6
PARTS = 2
CUTOFF = 1.0
SHIFT = 4.0
AXES = ("gx", "gy", "gz")
MESH = pl.DeviceIdType.MESH
F32 = jnp.float32
BF16 = jnp.bfloat16
NT = (((1,), (1,)), ((), ()))
NN = (((1,), (0,)), ((), ()))


def iota(shape, dim):
    return lax.broadcasted_iota(jnp.int32, shape, dim)


def split(a):
    high = a.astype(BF16)
    return high, (a - high.astype(F32)).astype(BF16)


def dot(a, b, dims=NN):
    return lax.dot_general(a, b, dims, preferred_element_type=F32)


def dot_full(a, b, dims=NN):
    return lax.dot_general(a, b, dims, precision=lax.Precision.HIGHEST, preferred_element_type=F32)


def dot3(a, b, dims=NN):
    rows = a[0].shape[0]
    both = dot(jnp.concatenate(a, axis=0), b[0], dims)
    return both[:rows] + (both[rows:] + dot(a[0], b[1], dims))


def dot2(a, b, dims=NN):
    rows = a.shape[0]
    both = dot(jnp.concatenate(split(a), axis=0), b, dims)
    return both[:rows] + both[rows:]


def dot2r(a, b, dims=NN):
    high, low = split(b)
    return dot(a, high, dims) + dot(a, low, dims)


def flag(condition, dtype=F32):
    return jnp.where(condition, 1.0, 0.0).astype(dtype)


def plane_matrix(width, first):
    cells = width * width

    def coordinates(lane):
        return lax.rem(lax.div(lane, width) + first, width), lax.rem(lane, width)

    (row_y, row_z), (col_y, col_z) = coordinates(iota((cells, 1), 0)), coordinates(iota((1, cells), 1))
    gap = jnp.abs(row_y - col_y) + jnp.abs(row_z - col_z)
    return jnp.where(gap == 0, 3.0 - SHIFT, jnp.where(gap == 1, -0.5, 0.0)).astype(BF16)


def max_stages(sizes):
    reach = [range(0, n, 2) for n in sizes]
    every = [o for o in itertools.product(*reach) if any(o)]
    if len(every) < 8:
        return [every]
    stages = []
    for axis in range(3):
        if len(reach[axis]) > 1:
            stages.append([tuple(d if k == axis else 0 for k in range(3)) for d in reach[axis][1:]])
    return stages


def kernel(
    length, sizes, orb_hbm, pot_hbm, coef_hbm, out_ref,
    matrix, pick, orb, pot, coef, tiles, tops, tops_in, wide, u, v, rest_faces, facet, ft_in, v_in, p_out, p_in,
    load_sem, tile_send, tile_recv, top_send, top_recv,
    v_send, v_recv, f_send, f_recv, p_send, p_recv,
):
    me = [lax.axis_index(a) for a in AXES]
    rows, cols = coef.shape
    doubled, area = 2 * length, length * length
    plane, lower = doubled * doubled, length // 2
    half = cols // PARTS

    moved = [[me[k]] + [lax.rem(me[k] + d, sizes[k]) for d in range(1, sizes[k])] for k in range(3)]

    def at(offset):
        return tuple(moved[k][offset[k] % sizes[k]] for k in range(3))

    def finish(region, sem):
        pltpu.make_async_copy(region, region, sem).wait()

    def remote(src, dst, send, recv, offset):
        return pltpu.make_async_remote_copy(
            src_ref=src, dst_ref=dst, send_sem=send, recv_sem=recv, device_id=at(offset), device_id_type=MESH
        )

    tile_slots = [s for s in itertools.product((0, 1), repeat=3) if s != (1, 1, 1)]
    tile_to = {s: tuple(1 - k for k in s) for s in tile_slots}
    stages = max_stages(sizes)
    faces = []
    for axis in range(3):
        for side in (-1, 1):
            faces.append(tuple(side if k == axis else 0 for k in range(3)))

    def wrapped(offset):
        return tuple(o % n for o, n in zip(offset, sizes))

    greeted = set()
    for offset in list(tile_to.values()) + sum(stages, []) + faces:
        greeted.add(wrapped(offset))
        greeted.add(wrapped(tuple(-o for o in offset)))
    greeted = sorted(greeted)

    barrier = pltpu.get_barrier_semaphore()
    for offset in greeted:
        pl.semaphore_signal(barrier, inc=1, device_id=at(offset), device_id_type=MESH)

    load_pot = pltpu.make_async_copy(pot_hbm, pot, load_sem.at[0])
    load_orb = pltpu.make_async_copy(
        orb_hbm.at[:, pl.ds((lower - 2) * plane, (length + 4) * plane)], orb, load_sem.at[1]
    )
    load_coef = pltpu.make_async_copy(coef_hbm, coef, load_sem.at[2])
    load_pot.start()
    load_orb.start()
    load_coef.start()

    matrix[...] = plane_matrix(doubled, lower)
    lanes = length * doubled
    cells = length * lanes
    cell = iota((1, cells), 1)
    inner = iota((area, 1), 0)
    major, minor = lax.div(inner, length), lax.rem(inner, length)
    for f in range(6):
        layer = (length - 1) * (f % 2)
        picked_cell = (
            layer * lanes + major * doubled + lower + minor,
            major * lanes + layer * doubled + lower + minor,
            major * lanes + minor * doubled + lower + layer,
        )[f // 2]
        pick[pl.ds(f * area, area), :] = flag(cell == picked_cell, BF16)

    load_pot.wait()
    flat = pot[...].reshape(area, length)
    spread = flag(lax.rem(iota((1, lanes), 1), doubled) == iota((length, 1), 0))
    keep = lax.div(iota((1, lanes), 1), doubled) == lax.rem(iota((area, 1), 0), length)
    spread_rows = jnp.where(keep, dot_full(flat, spread), 0.0)
    own = len(tile_slots)
    tiles[own] = jnp.sum(spread_rows.reshape(length, length, lanes), axis=1)

    pl.semaphore_wait(barrier, len(greeted))

    for s, slot in enumerate(tile_slots):
        copy = remote(tiles.at[own], tiles.at[s], tile_send, tile_recv, tile_to[slot])
        copy.start()

    load_coef.wait()
    v_copies = {}
    shared = [f for f in range(6) if f % 2 == 0 or sizes[f // 2] > 2]
    for k, f in enumerate(shared):
        v_copies[f] = remote(coef, v_in.at[k], v_send, v_recv, faces[f])
    for f in shared[:2]:
        v_copies[f].start()

    load_orb.wait()

    def w(i):
        return orb[:, pl.ds(pl.multiple_of(i * plane, plane), plane)]

    @pl.loop(0, length + 4, unroll=4)
    def _(i):
        here = pl.ds(pl.multiple_of(i * plane, plane), plane)
        orb[:, here] = pltpu.roll(orb[:, here], plane - lower * doubled, 1)

    @pl.loop(0, length + 2, unroll=5)
    def _(i):
        u[i] = dot2(w(i + 1), matrix[...]) - 0.5 * (w(i) + w(i + 2))

    finish(tiles.at[pl.ds(0, own)], tile_recv)
    for a in range(2):
        quarters = []
        for b in range(2):
            quarters.append(tiles[4 * a + 2 * b] + pltpu.roll(tiles[4 * a + 2 * b + 1], length, 1))
        wide[pl.ds(a * length, length), :] = pltpu.roll(
            jnp.concatenate(quarters, axis=1), plane - lower * doubled, 1
        )

    sent = 0

    def send_max(stage):
        for d, offset in enumerate(stages[stage]):
            k = sent + d
            copy = remote(
                tops.at[stage], tops_in.at[k], top_send.at[stage], top_recv.at[stage], offset
            )
            copy.start()

    def gather_max(stage):
        finish(tops_in.at[pl.ds(sent, len(stages[stage]))], top_recv.at[stage])
        return functools.reduce(
            jnp.maximum, [tops_in[sent + d] for d in range(len(stages[stage]))], tops[stage]
        )

    top = jnp.max(jnp.max(wide[...], axis=1, keepdims=True), axis=0, keepdims=True)
    tops[0] = jnp.broadcast_to(top, tops.shape[1:])
    send_max(0)

    def potential(x):
        return wide[pl.ds(x, 1), :]

    @pl.loop(0, length + 2)
    def _(i):
        u[i] = u[i] + potential(i + lower - 1) * w(i + 1)

    near = pl.ds(0, lanes)

    @pl.loop(0, length, unroll=4)
    def _(i):
        v[i] = (
            dot2(u[i + 1], matrix[:, near])
            + potential(i + lower)[:, :lanes] * u[i + 1, :, near]
            - 0.5 * (u[i, :, near] + u[i + 2, :, near])
        )

    for stage in range(1, len(stages)):
        tops[stage] = gather_max(stage - 1)
        sent += len(stages[stage - 1])
        send_max(stage)
    top = gather_max(len(stages) - 1)
    for f in shared[2:]:
        v_copies[f].start()

    top = top[0:1, 0:1] + 6.0
    centre = (top + CUTOFF) / 2.0
    width = (top - CUTOFF) / 2.0
    away = centre - SHIFT
    alpha = 2.0 / (width * width)
    beta = -2.0 * away * alpha
    gamma = away * away * alpha - 1.0

    z = lax.rem(iota((1, lanes), 1), doubled)
    inside = flag((z >= lower) & (z < lower + length))
    alpha, beta, gamma = alpha * inside, beta * inside, gamma * inside
    planes = []
    for i in range(length):
        planes.append(alpha * v[i] + beta * u[i + 1, :, near] + gamma * orb[:, pl.ds((i + 2) * plane, lanes)])
    r = jnp.concatenate(planes, axis=1)
    r_s = split(r)
    gram = dot3(r_s, r_s, NT)
    sigma = jnp.sqrt(jnp.sum(jnp.sum(gram * gram, axis=1, keepdims=True), axis=0, keepdims=True))
    eye = flag(iota((rows, rows), 0) == iota((rows, rows), 1))
    product = gram * (1.0 / sigma)

    def pick_face(f):
        here = pl.ds(pl.multiple_of(f * area, area), area)
        rest_faces[here, :] = dot(pick[here, :], r_s[0], NT) + dot(pick[here, :], r_s[1], NT)

    def newton(step, state):
        product, inverse = state
        factor = 1.5 * eye - 0.5 * product
        factor_s = split(factor)
        once = dot3(split(product), factor_s)
        inverse = dot3(split(inverse), factor_s)
        pick_face(step)
        return dot3(split(once), factor_s), inverse

    product, inverse = lax.fori_loop(0, NEWTON - 1, newton, (product, eye))
    for f in range(NEWTON - 1, 6):
        pick_face(f)
    inverse = dot3(split(inverse), split(1.5 * eye - 0.5 * product))
    root = inverse * lax.rsqrt(sigma)
    root_s = split(root)

    rest_faces_s = split(rest_faces[...])
    facet[...] = dot3(rest_faces_s, root_s, NT)
    face_copies = []
    for f, offset in enumerate(faces):
        if sizes[f // 2] > 2:
            face_copies.append((f, pl.ds(f * area, area), pl.ds((f ^ 1) * area, area), offset))
        elif f % 2 == 0:
            both = pl.ds(f * area, 2 * area)
            face_copies.append((f, both, both, offset))
    for f, here, there, offset in face_copies:
        copy = remote(facet.at[here, :], ft_in.at[there, :], f_send, f_recv, offset)
        copy.start()

    facet_s = split(facet[...])
    inverse_width = 1.0 / width
    slots = []
    for f in range(6):
        slots.append(rest_faces[pl.ds((f if sizes[f // 2] > 2 else f ^ 1) * area, area), :])
    slots_s = split(jnp.concatenate(slots, axis=0))
    couple = split((-0.5 * inverse_width) * dot3(root_s, slots_s, NT))
    own_potential = jnp.concatenate([wide[pl.ds(lower + k, 1), near] for k in range(length)], axis=1)
    around = pltpu.roll(r, 1, 1) + pltpu.roll(r, cells - 1, 1)
    for stride in (lanes, doubled):
        coordinate = lax.rem(lax.div(cell, stride), length)
        around = around + flag(coordinate > 0) * pltpu.roll(r, stride, 1)
        around = around + flag(coordinate < length - 1) * pltpu.roll(r, cells - stride, 1)
    boxed = (3.0 + own_potential) * r - 0.5 * around
    energy = dot3(split(boxed), r_s, NT)
    block = dot3(split(dot3(root_s, split(energy))), root_s, NT)
    diagonal = split(inverse_width * (block - centre * eye))

    prior = coef[...]
    current = dot3(diagonal, split(prior))
    finish(tiles.at[pl.ds(0, own)], tile_send)
    for stage in range(len(stages)):
        finish(tops_in.at[pl.ds(0, len(stages[stage]))], top_send.at[stage])
    finish(v_in.at[pl.ds(0, len(shared))], v_send)
    finish(v_in.at[pl.ds(0, len(shared))], v_recv)
    came = [split(v_in[shared.index(f ^ 1 if f ^ 1 in shared else f)]) for f in range(6)]
    carried = []
    finish(ft_in, f_recv)
    for f in range(6):
        carried.append(dot3(split(ft_in[pl.ds(f * area, area), :]), came[f]))
    current = current + dot3(couple, split(jnp.concatenate(carried, axis=0)))

    def send_projected(number, part, vectors):
        p_out[number, part] = dot3(facet_s, split(vectors))
        for f, here, there, offset in face_copies:
            copy = remote(
                p_out.at[number, part, here, :], p_in.at[number, part, there, :],
                p_send.at[number, part], p_recv.at[number, part], offset,
            )
            copy.start()

    prior = [prior[:, k * half : (k + 1) * half] for k in range(PARTS)]
    current = [current[:, k * half : (k + 1) * half] for k in range(PARTS)]
    for part in range(PARTS):
        send_projected(0, part, current[part])
    finish(facet, f_send)
    for number in range(2):
        following = []
        for part in range(PARTS):
            mine = 2.0 * dot3(diagonal, split(current[part])) - prior[part]
            if number == 1:
                finish(p_out.at[0, part], p_send.at[0, part])
            finish(p_in.at[number, part], p_recv.at[number, part])
            mine = mine + 2.0 * dot3(couple, split(p_in[number, part]))
            following.append(mine)
            if number == 0:
                send_projected(1, part, mine)
            else:
                out_ref[:, pl.ds(part * half, half)] = mine
        prior, current = current, following

    for part in range(PARTS):
        finish(p_out.at[1, part], p_send.at[1, part])


def per_device(sizes, orbitals, potential, coefficients):
    length = potential.shape[0]
    rows, cells = orbitals.shape[-2:]
    cols = coefficients.shape[-1]
    doubled, area = 2 * length, length * length
    plane, lanes = doubled * doubled, length * doubled
    stages = max_stages(sizes)
    top_copies = max(sum(len(stage) for stage in stages), 1)
    dma = pltpu.SemaphoreType.DMA
    result = pl.pallas_call(
        functools.partial(kernel, length, sizes),
        out_shape=jax.ShapeDtypeStruct((rows, cols), F32),
        in_specs=[pl.BlockSpec(memory_space=pltpu.HBM)] * 3,
        out_specs=pl.BlockSpec(memory_space=pltpu.VMEM),
        scratch_shapes=[
            pltpu.VMEM((plane, plane), BF16),
            pltpu.VMEM((6 * area, length * lanes), BF16),
            pltpu.VMEM((rows, (length + 4) * plane), F32),
            pltpu.VMEM((length, length, length), F32),
            pltpu.VMEM((rows, cols), F32),
            pltpu.VMEM((8, length, lanes), F32),
            pltpu.VMEM((len(stages), 8, 128), F32),
            pltpu.VMEM((top_copies, 8, 128), F32),
            pltpu.VMEM((doubled, plane), F32),
            pltpu.VMEM((length + 2, rows, plane), F32),
            pltpu.VMEM((length, rows, lanes), F32),
            pltpu.VMEM((6 * area, rows), F32),
            pltpu.VMEM((6 * area, rows), F32),
            pltpu.VMEM((6 * area, rows), F32),
            pltpu.VMEM((6, rows, cols), F32),
            pltpu.VMEM((2, PARTS, 6 * area, cols // PARTS), F32),
            pltpu.VMEM((2, PARTS, 6 * area, cols // PARTS), F32),
            dma((3,)),
            dma,
            dma,
            dma((max(len(stages), 1),)),
            dma((max(len(stages), 1),)),
            dma,
            dma,
            dma,
            dma,
            dma((2, PARTS)),
            dma((2, PARTS)),
        ],
        compiler_params=pltpu.CompilerParams(
            collective_id=0, has_side_effects=True, vmem_limit_bytes=60 * 1024 * 1024
        ),
    )(orbitals.reshape(rows, cells), potential, coefficients.reshape(rows, cols))
    return result.reshape(coefficients.shape)


def solution(mesh):
    sizes = tuple(mesh.shape[a] for a in AXES)
    placed = (P("gx", "gy", "gz", None, None), P("gx", "gy", "gz"), P("gx", "gy", "gz", None, None))
    return jax.shard_map(
        functools.partial(per_device, sizes),
        mesh=mesh,
        in_specs=placed,
        out_specs=P("gx", "gy", "gz", None, None),
        check_vma=False,
    )
```

```python
import functools
import itertools

import jax
import jax.numpy as jnp
from jax import lax
from jax.experimental import pallas as pl
from jax.experimental.pallas import tpu as pltpu
from jax.sharding import PartitionSpec as P

NEWTON = 6
PARTS = 2
CUTOFF = 1.0
SHIFT = 4.0
AXES = ("gx", "gy", "gz")
MESH = pl.DeviceIdType.MESH
F32 = jnp.float32
BF16 = jnp.bfloat16
NT = (((1,), (1,)), ((), ()))
NN = (((1,), (0,)), ((), ()))


def iota(shape, dim):
    return lax.broadcasted_iota(jnp.int32, shape, dim)


def split(a):
    high = a.astype(BF16)
    return high, (a - high.astype(F32)).astype(BF16)


def dot(a, b, dims=NN):
    return lax.dot_general(a, b, dims, preferred_element_type=F32)


def dot_full(a, b, dims=NN):
    return lax.dot_general(a, b, dims, precision=lax.Precision.HIGHEST, preferred_element_type=F32)


def dot3(a, b, dims=NN):
    rows = a[0].shape[0]
    both = dot(jnp.concatenate(a, axis=0), b[0], dims)
    return both[:rows] + (both[rows:] + dot(a[0], b[1], dims))


def dot2(a, b, dims=NN):
    rows = a.shape[0]
    both = dot(jnp.concatenate(split(a), axis=0), b, dims)
    return both[:rows] + both[rows:]


def dot2r(a, b, dims=NN):
    high, low = split(b)
    return dot(a, high, dims) + dot(a, low, dims)


def flag(condition, dtype=F32):
    return jnp.where(condition, 1.0, 0.0).astype(dtype)


def plane_matrix(width):
    cells = width * width
    row, col = iota((cells, 1), 0), iota((1, cells), 1)
    gap = row - col
    inside = lax.div(row, width) == lax.div(col, width)
    near = ((jnp.abs(gap) == 1) & inside) | (jnp.abs(gap) == width)
    return (jnp.where(gap == 0, 3.0 - SHIFT, 0.0) - 0.5 * flag(near)).astype(BF16)


def max_stages(sizes):
    reach = [range(0, n, 2) for n in sizes]
    every = [o for o in itertools.product(*reach) if any(o)]
    if len(every) < 8:
        return [every]
    stages = []
    for axis in range(3):
        if len(reach[axis]) > 1:
            stages.append([tuple(d if k == axis else 0 for k in range(3)) for d in reach[axis][1:]])
    return stages


def kernel(
    length, sizes, orb_hbm, pot_hbm, coef_hbm, out_ref,
    matrix, select, pick, orb, pot, coef, tiles, tops, tops_in, wide, u, v, own_w, own_u, own_v, rest_faces, facet, ft_in, v_in, p_out, p_in,
    load_sem, tile_send, tile_recv, top_send, top_recv,
    v_send, v_recv, f_send, f_recv, p_send, p_recv,
):
    me = [lax.axis_index(a) for a in AXES]
    rows, cols = coef.shape
    doubled, area = 2 * length, length * length
    plane, lower = doubled * doubled, length // 2
    half = cols // PARTS

    moved = [[me[k]] + [lax.rem(me[k] + d, sizes[k]) for d in range(1, sizes[k])] for k in range(3)]

    def at(offset):
        return tuple(moved[k][offset[k] % sizes[k]] for k in range(3))

    def finish(region, sem):
        pltpu.make_async_copy(region, region, sem).wait()

    def remote(src, dst, send, recv, offset):
        return pltpu.make_async_remote_copy(
            src_ref=src, dst_ref=dst, send_sem=send, recv_sem=recv, device_id=at(offset), device_id_type=MESH
        )

    tile_slots = [s for s in itertools.product((0, 1), repeat=3) if s != (1, 1, 1)]
    tile_to = {s: tuple(1 - k for k in s) for s in tile_slots}
    stages = max_stages(sizes)
    faces = []
    for axis in range(3):
        for side in (-1, 1):
            faces.append(tuple(side if k == axis else 0 for k in range(3)))

    def wrapped(offset):
        return tuple(o % n for o, n in zip(offset, sizes))

    greeted = set()
    for offset in list(tile_to.values()) + sum(stages, []) + faces:
        greeted.add(wrapped(offset))
        greeted.add(wrapped(tuple(-o for o in offset)))
    greeted = sorted(greeted)

    barrier = pltpu.get_barrier_semaphore()
    for offset in greeted:
        pl.semaphore_signal(barrier, inc=1, device_id=at(offset), device_id_type=MESH)

    load_pot = pltpu.make_async_copy(pot_hbm, pot, load_sem.at[0])
    load_orb = pltpu.make_async_copy(
        orb_hbm.at[:, pl.ds((lower - 2) * plane, (length + 4) * plane)], orb, load_sem.at[1]
    )
    load_coef = pltpu.make_async_copy(coef_hbm, coef, load_sem.at[2])
    load_pot.start()
    load_orb.start()
    load_coef.start()

    matrix[...] = plane_matrix(doubled)
    source, target = iota((plane, 1), 0), iota((1, 2 * area), 1)
    inner = lax.rem(target, area)
    wanted = (lower + lax.div(inner, length)) * doubled + lower + lax.rem(inner, length)
    for k in range(2):
        select[k] = flag(source == jnp.where(lax.div(target, area) == k, wanted, -1), BF16)
    cells = length * area
    cell = iota((1, cells), 1)
    for f in range(6):
        inner = iota((area, 1), 0)
        major, minor = lax.div(inner, length), lax.rem(inner, length)
        layer = (length - 1) * (f % 2)
        picked_cell = (
            layer * area + inner, major * area + layer * length + minor, major * area + minor * length + layer
        )[f // 2]
        pick[pl.ds(f * area, area), :] = flag(cell == picked_cell, BF16)

    load_pot.wait()
    lanes = length * doubled
    flat = pot[...].reshape(area, length)
    spread = flag(lax.rem(iota((1, lanes), 1), doubled) == iota((length, 1), 0))
    keep = lax.div(iota((1, lanes), 1), doubled) == lax.rem(iota((area, 1), 0), length)
    spread_rows = jnp.where(keep, dot_full(flat, spread), 0.0)
    own = len(tile_slots)
    tiles[own] = jnp.sum(spread_rows.reshape(length, length, lanes), axis=1)

    pl.semaphore_wait(barrier, len(greeted))

    for s, slot in enumerate(tile_slots):
        copy = remote(tiles.at[own], tiles.at[s], tile_send, tile_recv, tile_to[slot])
        copy.start()

    load_coef.wait()
    v_copies = {}
    shared = [f for f in range(6) if f % 2 == 0 or sizes[f // 2] > 2]
    for k, f in enumerate(shared):
        v_copies[f] = remote(coef, v_in.at[k], v_send, v_recv, faces[f])
    for f in shared[:2]:
        v_copies[f].start()

    load_orb.wait()

    def w(i):
        return orb[:, pl.ds(pl.multiple_of(i * plane, plane), plane)]

    def pair_lanes(pair):
        return pl.ds(pl.multiple_of(pair * 2 * area, 2 * area), 2 * area)

    def own_cells(even, odd):
        return dot2(even, select[0]) + dot2(odd, select[1])

    @pl.loop(0, length + 2, unroll=5)
    def _(i):
        u[i] = dot2(w(i + 1), matrix[...]) - 0.5 * (w(i) + w(i + 2))

    @pl.loop(0, length // 2, unroll=2)
    def _(pair):
        own_w[:, pair_lanes(pair)] = own_cells(w(2 * pair + 2), w(2 * pair + 3))

    finish(tiles.at[pl.ds(0, own)], tile_recv)
    for a in range(2):
        for b in range(2):
            low, high = tiles[4 * a + 2 * b], tiles[4 * a + 2 * b + 1]
            wide[pl.ds(a * length, length), pl.ds(b * lanes, lanes)] = low + pltpu.roll(high, length, 1)

    sent = 0

    def send_max(stage):
        for d, offset in enumerate(stages[stage]):
            k = sent + d
            copy = remote(
                tops.at[stage], tops_in.at[k], top_send.at[stage], top_recv.at[stage], offset
            )
            copy.start()

    def gather_max(stage):
        finish(tops_in.at[pl.ds(sent, len(stages[stage]))], top_recv.at[stage])
        return functools.reduce(
            jnp.maximum, [tops_in[sent + d] for d in range(len(stages[stage]))], tops[stage]
        )

    top = jnp.max(jnp.max(wide[...], axis=1, keepdims=True), axis=0, keepdims=True)
    tops[0] = jnp.broadcast_to(top, tops.shape[1:])
    send_max(0)

    def potential(x):
        return wide[pl.ds(x, 1), :]

    @pl.loop(0, length + 2)
    def _(i):
        u[i] = u[i] + potential(i + lower - 1) * w(i + 1)

    @pl.loop(0, length, unroll=4)
    def _(i):
        centre_plane = u[i + 1]
        v[i] = dot2(centre_plane, matrix[...]) + potential(i + lower) * centre_plane - 0.5 * (u[i] + u[i + 2])

    @pl.loop(0, length // 2, unroll=2)
    def _(pair):
        own_u[:, pair_lanes(pair)] = own_cells(u[2 * pair + 1], u[2 * pair + 2])
        own_v[:, pair_lanes(pair)] = own_cells(v[2 * pair], v[2 * pair + 1])

    for stage in range(1, len(stages)):
        tops[stage] = gather_max(stage - 1)
        sent += len(stages[stage - 1])
        send_max(stage)
    top = gather_max(len(stages) - 1)
    for f in shared[2:]:
        v_copies[f].start()

    top = top[0:1, 0:1] + 6.0
    centre = (top + CUTOFF) / 2.0
    width = (top - CUTOFF) / 2.0
    away = centre - SHIFT
    alpha = 2.0 / (width * width)
    beta = -2.0 * away * alpha
    gamma = away * away * alpha - 1.0

    r = alpha * own_v[...] + beta * own_u[...] + gamma * own_w[...]
    r_s = split(r)
    gram = dot3(r_s, r_s, NT)
    rest_faces[...] = dot(pick[...], r_s[0], NT) + dot(pick[...], r_s[1], NT)
    sigma = jnp.sqrt(jnp.sum(jnp.sum(gram * gram, axis=1, keepdims=True), axis=0, keepdims=True))
    eye = flag(iota((rows, rows), 0) == iota((rows, rows), 1))
    product = gram * (1.0 / sigma)

    def newton(step, state):
        product, inverse = state
        factor = 1.5 * eye - 0.5 * product
        factor_s = split(factor)
        once = dot3(split(product), factor_s)
        inverse = dot3(split(inverse), factor_s)
        return dot3(split(once), factor_s), inverse

    product, inverse = lax.fori_loop(0, NEWTON - 1, newton, (product, eye))
    inverse = dot3(split(inverse), split(1.5 * eye - 0.5 * product))
    root = inverse * lax.rsqrt(sigma)
    root_s = split(root)

    rest_faces_s = split(rest_faces[...])
    facet[...] = dot3(rest_faces_s, root_s, NT)
    face_copies = []
    for f, offset in enumerate(faces):
        if sizes[f // 2] > 2:
            face_copies.append((f, pl.ds(f * area, area), pl.ds((f ^ 1) * area, area), offset))
        elif f % 2 == 0:
            both = pl.ds(f * area, 2 * area)
            face_copies.append((f, both, both, offset))
    for f, here, there, offset in face_copies:
        copy = remote(facet.at[here, :], ft_in.at[there, :], f_send, f_recv, offset)
        copy.start()

    facet_s = split(facet[...])
    inverse_width = 1.0 / width
    slots = []
    for f in range(6):
        slots.append(rest_faces[pl.ds((f if sizes[f // 2] > 2 else f ^ 1) * area, area), :])
    slots_s = split(jnp.concatenate(slots, axis=0))
    couple = split((-0.5 * inverse_width) * dot3(root_s, slots_s, NT))
    own_wide = dot2(wide[pl.ds(lower, length), :], select[0])
    own_odd = pltpu.roll(own_wide, area, 1)
    own_potential = jnp.concatenate(
        [own_wide[k : k + 1, :] + own_odd[k + 1 : k + 2, :] for k in range(0, length, 2)], axis=1
    )
    around = jnp.zeros_like(r)
    for stride in (area, length, 1):
        coordinate = lax.rem(lax.div(cell, stride), length)
        around = around + flag(coordinate > 0) * pltpu.roll(r, stride, 1)
        around = around + flag(coordinate < length - 1) * pltpu.roll(r, cells - stride, 1)
    boxed = (3.0 + own_potential) * r - 0.5 * around
    energy = dot3(split(boxed), r_s, NT)
    block = dot3(split(dot3(root_s, split(energy))), root_s, NT)
    diagonal = split(inverse_width * (block - centre * eye))

    prior = coef[...]
    current = dot3(diagonal, split(prior))
    finish(tiles.at[pl.ds(0, own)], tile_send)
    for stage in range(len(stages)):
        finish(tops_in.at[pl.ds(0, len(stages[stage]))], top_send.at[stage])
    finish(v_in.at[pl.ds(0, len(shared))], v_send)
    finish(v_in.at[pl.ds(0, len(shared))], v_recv)
    came = [split(v_in[shared.index(f ^ 1 if f ^ 1 in shared else f)]) for f in range(6)]
    carried = []
    finish(ft_in, f_recv)
    for f in range(6):
        carried.append(dot3(split(ft_in[pl.ds(f * area, area), :]), came[f]))
    current = current + dot3(couple, split(jnp.concatenate(carried, axis=0)))

    def send_projected(number, part, vectors):
        p_out[number, part] = dot3(facet_s, split(vectors))
        for f, here, there, offset in face_copies:
            copy = remote(
                p_out.at[number, part, here, :], p_in.at[number, part, there, :],
                p_send.at[number, part], p_recv.at[number, part], offset,
            )
            copy.start()

    prior = [prior[:, k * half : (k + 1) * half] for k in range(PARTS)]
    current = [current[:, k * half : (k + 1) * half] for k in range(PARTS)]
    for part in range(PARTS):
        send_projected(0, part, current[part])
    finish(facet, f_send)
    for number in range(2):
        following = []
        for part in range(PARTS):
            mine = 2.0 * dot3(diagonal, split(current[part])) - prior[part]
            if number == 1:
                finish(p_out.at[0, part], p_send.at[0, part])
            finish(p_in.at[number, part], p_recv.at[number, part])
            mine = mine + 2.0 * dot3(couple, split(p_in[number, part]))
            following.append(mine)
            if number == 0:
                send_projected(1, part, mine)
            else:
                out_ref[:, pl.ds(part * half, half)] = mine
        prior, current = current, following

    for part in range(PARTS):
        finish(p_out.at[1, part], p_send.at[1, part])


def per_device(sizes, orbitals, potential, coefficients):
    length = potential.shape[0]
    rows, cells = orbitals.shape[-2:]
    cols = coefficients.shape[-1]
    doubled, area = 2 * length, length * length
    plane, lanes = doubled * doubled, length * doubled
    stages = max_stages(sizes)
    top_copies = max(sum(len(stage) for stage in stages), 1)
    dma = pltpu.SemaphoreType.DMA
    result = pl.pallas_call(
        functools.partial(kernel, length, sizes),
        out_shape=jax.ShapeDtypeStruct((rows, cols), F32),
        in_specs=[pl.BlockSpec(memory_space=pltpu.HBM)] * 3,
        out_specs=pl.BlockSpec(memory_space=pltpu.VMEM),
        scratch_shapes=[
            pltpu.VMEM((plane, plane), BF16),
            pltpu.VMEM((2, plane, 2 * area), BF16),
            pltpu.VMEM((6 * area, length * area), BF16),
            pltpu.VMEM((rows, (length + 4) * plane), F32),
            pltpu.VMEM((length, length, length), F32),
            pltpu.VMEM((rows, cols), F32),
            pltpu.VMEM((8, length, lanes), F32),
            pltpu.VMEM((len(stages), 8, 128), F32),
            pltpu.VMEM((top_copies, 8, 128), F32),
            pltpu.VMEM((doubled, plane), F32),
            pltpu.VMEM((length + 2, rows, plane), F32),
            pltpu.VMEM((length, rows, plane), F32),
            pltpu.VMEM((rows, length * area), F32),
            pltpu.VMEM((rows, length * area), F32),
            pltpu.VMEM((rows, length * area), F32),
            pltpu.VMEM((6 * area, rows), F32),
            pltpu.VMEM((6 * area, rows), F32),
            pltpu.VMEM((6 * area, rows), F32),
            pltpu.VMEM((6, rows, cols), F32),
            pltpu.VMEM((2, PARTS, 6 * area, cols // PARTS), F32),
            pltpu.VMEM((2, PARTS, 6 * area, cols // PARTS), F32),
            dma((3,)),
            dma,
            dma,
            dma((max(len(stages), 1),)),
            dma((max(len(stages), 1),)),
            dma,
            dma,
            dma,
            dma,
            dma((2, PARTS)),
            dma((2, PARTS)),
        ],
        compiler_params=pltpu.CompilerParams(
            collective_id=0, has_side_effects=True, vmem_limit_bytes=60 * 1024 * 1024
        ),
    )(orbitals.reshape(rows, cells), potential, coefficients.reshape(rows, cols))
    return result.reshape(coefficients.shape)


def solution(mesh):
    sizes = tuple(mesh.shape[a] for a in AXES)
    placed = (P("gx", "gy", "gz", None, None), P("gx", "gy", "gz"), P("gx", "gy", "gz", None, None))
    return jax.shard_map(
        functools.partial(per_device, sizes),
        mesh=mesh,
        in_specs=placed,
        out_specs=P("gx", "gy", "gz", None, None),
        check_vma=False,
    )
```

```python
import functools
import itertools

import jax
import jax.numpy as jnp
from jax import lax
from jax.experimental import pallas as pl
from jax.experimental.pallas import tpu as pltpu
from jax.sharding import PartitionSpec as P

NEWTON = 6
PARTS = 2
CUTOFF = 1.0
SHIFT = 4.0
AXES = ("gx", "gy", "gz")
MESH = pl.DeviceIdType.MESH
F32 = jnp.float32
BF16 = jnp.bfloat16
NT = (((1,), (1,)), ((), ()))
NN = (((1,), (0,)), ((), ()))


def iota(shape, dim):
    return lax.broadcasted_iota(jnp.int32, shape, dim)


def split(a):
    high = a.astype(BF16)
    return high, (a - high.astype(F32)).astype(BF16)


def dot(a, b, dims=NN):
    return lax.dot_general(a, b, dims, preferred_element_type=F32)


def dot_full(a, b, dims=NN):
    return lax.dot_general(a, b, dims, precision=lax.Precision.HIGHEST, preferred_element_type=F32)


def dot3(a, b, dims=NN):
    rows = a[0].shape[0]
    both = dot(jnp.concatenate(a, axis=0), b[0], dims)
    return both[:rows] + (both[rows:] + dot(a[0], b[1], dims))


def dot2(a, b, dims=NN):
    rows = a.shape[0]
    both = dot(jnp.concatenate(split(a), axis=0), b, dims)
    return both[:rows] + both[rows:]


def dot2r(a, b, dims=NN):
    high, low = split(b)
    return dot(a, high, dims) + dot(a, low, dims)


def flag(condition, dtype=F32):
    return jnp.where(condition, 1.0, 0.0).astype(dtype)


def plane_matrix(width):
    cells = width * width
    row, col = iota((cells, 1), 0), iota((1, cells), 1)
    gap = row - col
    inside = lax.div(row, width) == lax.div(col, width)
    near = ((jnp.abs(gap) == 1) & inside) | (jnp.abs(gap) == width)
    return (jnp.where(gap == 0, 3.0 - SHIFT, 0.0) - 0.5 * flag(near)).astype(BF16)


def max_stages(sizes):
    reach = [range(0, n, 2) for n in sizes]
    every = [o for o in itertools.product(*reach) if any(o)]
    if len(every) < 8:
        return [every]
    stages = []
    for axis in range(3):
        if len(reach[axis]) > 1:
            stages.append([tuple(d if k == axis else 0 for k in range(3)) for d in reach[axis][1:]])
    return stages


def kernel(
    length, sizes, orb_hbm, pot_hbm, coef_hbm, out_ref,
    matrix, select, pick, orb, pot, coef, tiles, tops, tops_in, wide, u, v, own_w, own_u, own_v, rest_faces, facet, ft_in, v_in, p_out, p_in,
    load_sem, tile_send, tile_recv, top_send, top_recv,
    v_send, v_recv, f_send, f_recv, p_send, p_recv,
):
    me = [lax.axis_index(a) for a in AXES]
    rows, cols = coef.shape
    doubled, area = 2 * length, length * length
    plane, lower = doubled * doubled, length // 2
    half = cols // PARTS

    moved = [[me[k]] + [lax.rem(me[k] + d, sizes[k]) for d in range(1, sizes[k])] for k in range(3)]

    def at(offset):
        return tuple(moved[k][offset[k] % sizes[k]] for k in range(3))

    def finish(region, sem):
        pltpu.make_async_copy(region, region, sem).wait()

    def remote(src, dst, send, recv, offset):
        return pltpu.make_async_remote_copy(
            src_ref=src, dst_ref=dst, send_sem=send, recv_sem=recv, device_id=at(offset), device_id_type=MESH
        )

    tile_slots = [s for s in itertools.product((0, 1), repeat=3) if s != (1, 1, 1)]
    tile_to = {s: tuple(1 - k for k in s) for s in tile_slots}
    stages = max_stages(sizes)
    faces = []
    for axis in range(3):
        for side in (-1, 1):
            faces.append(tuple(side if k == axis else 0 for k in range(3)))

    def wrapped(offset):
        return tuple(o % n for o, n in zip(offset, sizes))

    greeted = set()
    for offset in list(tile_to.values()) + sum(stages, []) + faces:
        greeted.add(wrapped(offset))
        greeted.add(wrapped(tuple(-o for o in offset)))
    greeted = sorted(greeted)

    barrier = pltpu.get_barrier_semaphore()
    for offset in greeted:
        pl.semaphore_signal(barrier, inc=1, device_id=at(offset), device_id_type=MESH)

    load_pot = pltpu.make_async_copy(pot_hbm, pot, load_sem.at[0])
    load_orb = pltpu.make_async_copy(
        orb_hbm.at[:, pl.ds((lower - 2) * plane, (length + 4) * plane)], orb, load_sem.at[1]
    )
    load_coef = pltpu.make_async_copy(coef_hbm, coef, load_sem.at[2])
    load_pot.start()
    load_orb.start()
    load_coef.start()

    matrix[...] = plane_matrix(doubled)
    source, target = iota((plane, 1), 0), iota((1, 2 * area), 1)
    inner = lax.rem(target, area)
    wanted = (lower + lax.div(inner, length)) * doubled + lower + lax.rem(inner, length)
    for k in range(2):
        select[k] = flag(source == jnp.where(lax.div(target, area) == k, wanted, -1), BF16)
    cells = length * area
    cell = iota((1, cells), 1)
    for f in range(6):
        inner = iota((area, 1), 0)
        major, minor = lax.div(inner, length), lax.rem(inner, length)
        layer = (length - 1) * (f % 2)
        picked_cell = (
            layer * area + inner, major * area + layer * length + minor, major * area + minor * length + layer
        )[f // 2]
        pick[pl.ds(f * area, area), :] = flag(cell == picked_cell, BF16)

    load_pot.wait()
    lanes = length * doubled
    flat = pot[...].reshape(area, length)
    spread = flag(lax.rem(iota((1, lanes), 1), doubled) == iota((length, 1), 0))
    keep = lax.div(iota((1, lanes), 1), doubled) == lax.rem(iota((area, 1), 0), length)
    spread_rows = jnp.where(keep, dot_full(flat, spread), 0.0)
    own = len(tile_slots)
    tiles[own] = jnp.sum(spread_rows.reshape(length, length, lanes), axis=1)

    pl.semaphore_wait(barrier, len(greeted))

    for s, slot in enumerate(tile_slots):
        copy = remote(tiles.at[own], tiles.at[s], tile_send, tile_recv, tile_to[slot])
        copy.start()

    load_coef.wait()
    v_copies = {}
    shared = [f for f in range(6) if f % 2 == 0 or sizes[f // 2] > 2]
    for k, f in enumerate(shared):
        v_copies[f] = remote(coef, v_in.at[k], v_send, v_recv, faces[f])

    load_orb.wait()

    def w(i):
        return orb[:, pl.ds(pl.multiple_of(i * plane, plane), plane)]

    def pair_lanes(pair):
        return pl.ds(pl.multiple_of(pair * 2 * area, 2 * area), 2 * area)

    def own_cells(even, odd):
        return dot2(even, select[0]) + dot2(odd, select[1])

    @pl.loop(0, length + 2, unroll=5)
    def _(i):
        u[i] = dot2(w(i + 1), matrix[...]) - 0.5 * (w(i) + w(i + 2))

    @pl.loop(0, length // 2, unroll=2)
    def _(pair):
        own_w[:, pair_lanes(pair)] = own_cells(w(2 * pair + 2), w(2 * pair + 3))

    finish(tiles.at[pl.ds(0, own)], tile_recv)
    for a in range(2):
        for b in range(2):
            low, high = tiles[4 * a + 2 * b], tiles[4 * a + 2 * b + 1]
            wide[pl.ds(a * length, length), pl.ds(b * lanes, lanes)] = low + pltpu.roll(high, length, 1)

    sent = 0

    def send_max(stage):
        for d, offset in enumerate(stages[stage]):
            k = sent + d
            copy = remote(
                tops.at[stage], tops_in.at[k], top_send.at[stage], top_recv.at[stage], offset
            )
            copy.start()

    def gather_max(stage):
        finish(tops_in.at[pl.ds(sent, len(stages[stage]))], top_recv.at[stage])
        return functools.reduce(
            jnp.maximum, [tops_in[sent + d] for d in range(len(stages[stage]))], tops[stage]
        )

    top = jnp.max(jnp.max(wide[...], axis=1, keepdims=True), axis=0, keepdims=True)
    tops[0] = jnp.broadcast_to(top, tops.shape[1:])
    send_max(0)

    def potential(x):
        return wide[pl.ds(x, 1), :]

    @pl.loop(0, length + 2)
    def _(i):
        u[i] = u[i] + potential(i + lower - 1) * w(i + 1)

    @pl.loop(0, length, unroll=4)
    def _(i):
        centre_plane = u[i + 1]
        v[i] = dot2(centre_plane, matrix[...]) + potential(i + lower) * centre_plane - 0.5 * (u[i] + u[i + 2])

    @pl.loop(0, length // 2, unroll=2)
    def _(pair):
        own_u[:, pair_lanes(pair)] = own_cells(u[2 * pair + 1], u[2 * pair + 2])
        own_v[:, pair_lanes(pair)] = own_cells(v[2 * pair], v[2 * pair + 1])

    for stage in range(1, len(stages)):
        tops[stage] = gather_max(stage - 1)
        sent += len(stages[stage - 1])
        send_max(stage)
    top = gather_max(len(stages) - 1)
    for f in shared:
        v_copies[f].start()

    top = top[0:1, 0:1] + 6.0
    centre = (top + CUTOFF) / 2.0
    width = (top - CUTOFF) / 2.0
    away = centre - SHIFT
    alpha = 2.0 / (width * width)
    beta = -2.0 * away * alpha
    gamma = away * away * alpha - 1.0

    r = alpha * own_v[...] + beta * own_u[...] + gamma * own_w[...]
    r_s = split(r)
    gram = dot3(r_s, r_s, NT)
    rest_faces[...] = dot(pick[...], r_s[0], NT) + dot(pick[...], r_s[1], NT)
    sigma = jnp.sqrt(jnp.sum(jnp.sum(gram * gram, axis=1, keepdims=True), axis=0, keepdims=True))
    eye = flag(iota((rows, rows), 0) == iota((rows, rows), 1))
    product = gram * (1.0 / sigma)

    def newton(step, state):
        product, inverse = state
        factor = 1.5 * eye - 0.5 * product
        factor_s = split(factor)
        once = dot3(split(product), factor_s)
        inverse = dot3(split(inverse), factor_s)
        return dot3(split(once), factor_s), inverse

    product, inverse = lax.fori_loop(0, NEWTON - 1, newton, (product, eye))
    inverse = dot3(split(inverse), split(1.5 * eye - 0.5 * product))
    root = inverse * lax.rsqrt(sigma)
    root_s = split(root)

    rest_faces_s = split(rest_faces[...])
    facet[...] = dot3(rest_faces_s, root_s, NT)
    face_copies = []
    for f, offset in enumerate(faces):
        if sizes[f // 2] > 2:
            face_copies.append((f, pl.ds(f * area, area), pl.ds((f ^ 1) * area, area), offset))
        elif f % 2 == 0:
            both = pl.ds(f * area, 2 * area)
            face_copies.append((f, both, both, offset))
    for f, here, there, offset in face_copies:
        copy = remote(facet.at[here, :], ft_in.at[there, :], f_send, f_recv, offset)
        copy.start()

    facet_s = split(facet[...])
    inverse_width = 1.0 / width
    slots = []
    for f in range(6):
        slots.append(rest_faces[pl.ds((f if sizes[f // 2] > 2 else f ^ 1) * area, area), :])
    slots_s = split(jnp.concatenate(slots, axis=0))
    couple = split((-0.5 * inverse_width) * dot3(root_s, slots_s, NT))
    own_wide = dot2(wide[pl.ds(lower, length), :], select[0])
    own_odd = pltpu.roll(own_wide, area, 1)
    own_potential = jnp.concatenate(
        [own_wide[k : k + 1, :] + own_odd[k + 1 : k + 2, :] for k in range(0, length, 2)], axis=1
    )
    around = jnp.zeros_like(r)
    for stride in (area, length, 1):
        coordinate = lax.rem(lax.div(cell, stride), length)
        around = around + flag(coordinate > 0) * pltpu.roll(r, stride, 1)
        around = around + flag(coordinate < length - 1) * pltpu.roll(r, cells - stride, 1)
    boxed = (3.0 + own_potential) * r - 0.5 * around
    energy = dot3(split(boxed), r_s, NT)
    block = dot3(split(dot3(root_s, split(energy))), root_s, NT)
    diagonal = split(inverse_width * (block - centre * eye))

    prior = coef[...]
    current = dot3(diagonal, split(prior))
    finish(tiles.at[pl.ds(0, own)], tile_send)
    for stage in range(len(stages)):
        finish(tops_in.at[pl.ds(0, len(stages[stage]))], top_send.at[stage])
    finish(v_in.at[pl.ds(0, len(shared))], v_send)
    finish(v_in.at[pl.ds(0, len(shared))], v_recv)
    came = [split(v_in[shared.index(f ^ 1 if f ^ 1 in shared else f)]) for f in range(6)]
    carried = []
    finish(ft_in, f_recv)
    for f in range(6):
        carried.append(dot3(split(ft_in[pl.ds(f * area, area), :]), came[f]))
    current = current + dot3(couple, split(jnp.concatenate(carried, axis=0)))

    def send_projected(number, part, vectors):
        p_out[number, part] = dot3(facet_s, split(vectors))
        for f, here, there, offset in face_copies:
            copy = remote(
                p_out.at[number, part, here, :], p_in.at[number, part, there, :],
                p_send.at[number, part], p_recv.at[number, part], offset,
            )
            copy.start()

    prior = [prior[:, k * half : (k + 1) * half] for k in range(PARTS)]
    current = [current[:, k * half : (k + 1) * half] for k in range(PARTS)]
    for part in range(PARTS):
        send_projected(0, part, current[part])
    finish(facet, f_send)
    for number in range(2):
        following = []
        for part in range(PARTS):
            mine = 2.0 * dot3(diagonal, split(current[part])) - prior[part]
            if number == 1:
                finish(p_out.at[0, part], p_send.at[0, part])
            finish(p_in.at[number, part], p_recv.at[number, part])
            mine = mine + 2.0 * dot3(couple, split(p_in[number, part]))
            following.append(mine)
            if number == 0:
                send_projected(1, part, mine)
            else:
                out_ref[:, pl.ds(part * half, half)] = mine
        prior, current = current, following

    for part in range(PARTS):
        finish(p_out.at[1, part], p_send.at[1, part])


def per_device(sizes, orbitals, potential, coefficients):
    length = potential.shape[0]
    rows, cells = orbitals.shape[-2:]
    cols = coefficients.shape[-1]
    doubled, area = 2 * length, length * length
    plane, lanes = doubled * doubled, length * doubled
    stages = max_stages(sizes)
    top_copies = max(sum(len(stage) for stage in stages), 1)
    dma = pltpu.SemaphoreType.DMA
    result = pl.pallas_call(
        functools.partial(kernel, length, sizes),
        out_shape=jax.ShapeDtypeStruct((rows, cols), F32),
        in_specs=[pl.BlockSpec(memory_space=pltpu.HBM)] * 3,
        out_specs=pl.BlockSpec(memory_space=pltpu.VMEM),
        scratch_shapes=[
            pltpu.VMEM((plane, plane), BF16),
            pltpu.VMEM((2, plane, 2 * area), BF16),
            pltpu.VMEM((6 * area, length * area), BF16),
            pltpu.VMEM((rows, (length + 4) * plane), F32),
            pltpu.VMEM((length, length, length), F32),
            pltpu.VMEM((rows, cols), F32),
            pltpu.VMEM((8, length, lanes), F32),
            pltpu.VMEM((len(stages), 8, 128), F32),
            pltpu.VMEM((top_copies, 8, 128), F32),
            pltpu.VMEM((doubled, plane), F32),
            pltpu.VMEM((length + 2, rows, plane), F32),
            pltpu.VMEM((length, rows, plane), F32),
            pltpu.VMEM((rows, length * area), F32),
            pltpu.VMEM((rows, length * area), F32),
            pltpu.VMEM((rows, length * area), F32),
            pltpu.VMEM((6 * area, rows), F32),
            pltpu.VMEM((6 * area, rows), F32),
            pltpu.VMEM((6 * area, rows), F32),
            pltpu.VMEM((6, rows, cols), F32),
            pltpu.VMEM((2, PARTS, 6 * area, cols // PARTS), F32),
            pltpu.VMEM((2, PARTS, 6 * area, cols // PARTS), F32),
            dma((3,)),
            dma,
            dma,
            dma((max(len(stages), 1),)),
            dma((max(len(stages), 1),)),
            dma,
            dma,
            dma,
            dma,
            dma((2, PARTS)),
            dma((2, PARTS)),
        ],
        compiler_params=pltpu.CompilerParams(
            collective_id=0, has_side_effects=True, vmem_limit_bytes=60 * 1024 * 1024
        ),
    )(orbitals.reshape(rows, cells), potential, coefficients.reshape(rows, cols))
    return result.reshape(coefficients.shape)


def solution(mesh):
    sizes = tuple(mesh.shape[a] for a in AXES)
    placed = (P("gx", "gy", "gz", None, None), P("gx", "gy", "gz"), P("gx", "gy", "gz", None, None))
    return jax.shard_map(
        functools.partial(per_device, sizes),
        mesh=mesh,
        in_specs=placed,
        out_specs=P("gx", "gy", "gz", None, None),
        check_vma=False,
    )
```

```python
import functools
import itertools

import jax
import jax.numpy as jnp
from jax import lax
from jax.experimental import pallas as pl
from jax.experimental.pallas import tpu as pltpu
from jax.sharding import PartitionSpec as P

NEWTON = 6
PARTS = 2
CUTOFF = 1.0
SHIFT = 4.0
AXES = ("gx", "gy", "gz")
MESH = pl.DeviceIdType.MESH
F32 = jnp.float32
BF16 = jnp.bfloat16
NT = (((1,), (1,)), ((), ()))
NN = (((1,), (0,)), ((), ()))


def iota(shape, dim):
    return lax.broadcasted_iota(jnp.int32, shape, dim)


def split(a):
    high = a.astype(BF16)
    return high, (a - high.astype(F32)).astype(BF16)


def dot(a, b, dims=NN):
    return lax.dot_general(a, b, dims, preferred_element_type=F32)


def dot_full(a, b, dims=NN):
    return lax.dot_general(a, b, dims, precision=lax.Precision.HIGHEST, preferred_element_type=F32)


def dot3(a, b, dims=NN):
    rows = a[0].shape[0]
    both = dot(jnp.concatenate(a, axis=0), b[0], dims)
    return both[:rows] + (both[rows:] + dot(a[0], b[1], dims))


def dot2(a, b, dims=NN):
    rows = a.shape[0]
    both = dot(jnp.concatenate(split(a), axis=0), b, dims)
    return both[:rows] + both[rows:]


def dot2r(a, b, dims=NN):
    high, low = split(b)
    return dot(a, high, dims) + dot(a, low, dims)


def flag(condition, dtype=F32):
    return jnp.where(condition, 1.0, 0.0).astype(dtype)


def plane_matrix(width):
    cells = width * width
    row, col = iota((cells, 1), 0), iota((1, cells), 1)
    gap = row - col
    inside = lax.div(row, width) == lax.div(col, width)
    near = ((jnp.abs(gap) == 1) & inside) | (jnp.abs(gap) == width)
    return (jnp.where(gap == 0, 3.0 - SHIFT, 0.0) - 0.5 * flag(near)).astype(BF16)


def max_stages(sizes):
    reach = [range(0, n, 2) for n in sizes]
    every = [o for o in itertools.product(*reach) if any(o)]
    if len(every) < 8:
        return [every]
    stages = []
    for axis in range(3):
        if len(reach[axis]) > 1:
            stages.append([tuple(d if k == axis else 0 for k in range(3)) for d in reach[axis][1:]])
    return stages


def kernel(
    length, sizes, orb_hbm, pot_hbm, coef_hbm, out_ref,
    matrix, select, pick, orb, pot, coef, tiles, tops, tops_in, wide, u, v, own_w, own_u, own_v, rest_faces, facet, ft_in, v_in, p_out, p_in,
    load_sem, tile_send, tile_recv, top_send, top_recv,
    v_send, v_recv, f_send, f_recv, p_send, p_recv,
):
    me = [lax.axis_index(a) for a in AXES]
    rows, cols = coef.shape
    doubled, area = 2 * length, length * length
    plane, lower = doubled * doubled, length // 2
    half = cols // PARTS

    moved = [[me[k]] + [lax.rem(me[k] + d, sizes[k]) for d in range(1, sizes[k])] for k in range(3)]

    def at(offset):
        return tuple(moved[k][offset[k] % sizes[k]] for k in range(3))

    def finish(region, sem):
        pltpu.make_async_copy(region, region, sem).wait()

    def remote(src, dst, send, recv, offset):
        return pltpu.make_async_remote_copy(
            src_ref=src, dst_ref=dst, send_sem=send, recv_sem=recv, device_id=at(offset), device_id_type=MESH
        )

    tile_slots = [s for s in itertools.product((0, 1), repeat=3) if s != (1, 1, 1)]
    tile_to = {s: tuple(1 - k for k in s) for s in tile_slots}
    stages = max_stages(sizes)
    faces = []
    for axis in range(3):
        for side in (-1, 1):
            faces.append(tuple(side if k == axis else 0 for k in range(3)))

    def wrapped(offset):
        return tuple(o % n for o, n in zip(offset, sizes))

    greeted = set()
    for offset in list(tile_to.values()) + sum(stages, []) + faces:
        greeted.add(wrapped(offset))
        greeted.add(wrapped(tuple(-o for o in offset)))
    greeted = sorted(greeted)

    barrier = pltpu.get_barrier_semaphore()
    for offset in greeted:
        pl.semaphore_signal(barrier, inc=1, device_id=at(offset), device_id_type=MESH)

    load_pot = pltpu.make_async_copy(pot_hbm, pot, load_sem.at[0])
    load_orb = pltpu.make_async_copy(
        orb_hbm.at[:, pl.ds((lower - 2) * plane, (length + 4) * plane)], orb, load_sem.at[1]
    )
    load_coef = pltpu.make_async_copy(coef_hbm, coef, load_sem.at[2])
    load_pot.start()
    load_orb.start()
    load_coef.start()

    matrix[...] = plane_matrix(doubled)
    source, target = iota((plane, 1), 0), iota((1, 2 * area), 1)
    inner = lax.rem(target, area)
    wanted = (lower + lax.div(inner, length)) * doubled + lower + lax.rem(inner, length)
    for k in range(2):
        select[k] = flag(source == jnp.where(lax.div(target, area) == k, wanted, -1), BF16)
    cells = length * area
    cell = iota((1, cells), 1)
    for f in range(6):
        inner = iota((area, 1), 0)
        major, minor = lax.div(inner, length), lax.rem(inner, length)
        layer = (length - 1) * (f % 2)
        picked_cell = (
            layer * area + inner, major * area + layer * length + minor, major * area + minor * length + layer
        )[f // 2]
        pick[pl.ds(f * area, area), :] = flag(cell == picked_cell, BF16)

    load_pot.wait()
    lanes = length * doubled
    flat = pot[...].reshape(area, length)
    spread = flag(lax.rem(iota((1, lanes), 1), doubled) == iota((length, 1), 0))
    keep = lax.div(iota((1, lanes), 1), doubled) == lax.rem(iota((area, 1), 0), length)
    spread_rows = jnp.where(keep, dot_full(flat, spread), 0.0)
    own = len(tile_slots)
    tiles[own] = jnp.sum(spread_rows.reshape(length, length, lanes), axis=1)

    pl.semaphore_wait(barrier, len(greeted))

    for s, slot in enumerate(tile_slots):
        copy = remote(tiles.at[own], tiles.at[s], tile_send, tile_recv, tile_to[slot])
        copy.start()

    load_coef.wait()
    v_copies = {}
    shared = [f for f in range(6) if f % 2 == 0 or sizes[f // 2] > 2]
    for k, f in enumerate(shared):
        v_copies[f] = remote(coef, v_in.at[k], v_send, v_recv, faces[f])
    for f in shared[:2]:
        v_copies[f].start()

    load_orb.wait()

    def w(i):
        return orb[:, pl.ds(pl.multiple_of(i * plane, plane), plane)]

    def pair_lanes(pair):
        return pl.ds(pl.multiple_of(pair * 2 * area, 2 * area), 2 * area)

    def own_cells(even, odd):
        return dot2(even, select[0]) + dot2(odd, select[1])

    @pl.loop(0, length + 2, unroll=5)
    def _(i):
        u[i] = dot2(w(i + 1), matrix[...]) - 0.5 * (w(i) + w(i + 2))

    finish(tiles.at[pl.ds(0, own)], tile_recv)
    for a in range(2):
        for b in range(2):
            low, high = tiles[4 * a + 2 * b], tiles[4 * a + 2 * b + 1]
            wide[pl.ds(a * length, length), pl.ds(b * lanes, lanes)] = low + pltpu.roll(high, length, 1)

    sent = 0

    def send_max(stage):
        for d, offset in enumerate(stages[stage]):
            k = sent + d
            copy = remote(
                tops.at[stage], tops_in.at[k], top_send.at[stage], top_recv.at[stage], offset
            )
            copy.start()

    def gather_max(stage):
        finish(tops_in.at[pl.ds(sent, len(stages[stage]))], top_recv.at[stage])
        return functools.reduce(
            jnp.maximum, [tops_in[sent + d] for d in range(len(stages[stage]))], tops[stage]
        )

    top = jnp.max(jnp.max(wide[...], axis=1, keepdims=True), axis=0, keepdims=True)
    tops[0] = jnp.broadcast_to(top, tops.shape[1:])
    send_max(0)

    def potential(x):
        return wide[pl.ds(x, 1), :]

    @pl.loop(0, length + 2)
    def _(i):
        u[i] = u[i] + potential(i + lower - 1) * w(i + 1)

    @pl.loop(0, length, unroll=4)
    def _(i):
        centre_plane = u[i + 1]
        v[i] = dot2(centre_plane, matrix[...]) + potential(i + lower) * centre_plane - 0.5 * (u[i] + u[i + 2])

    @pl.loop(0, length // 2, unroll=2)
    def _(pair):
        own_w[:, pair_lanes(pair)] = own_cells(w(2 * pair + 2), w(2 * pair + 3))
        own_u[:, pair_lanes(pair)] = own_cells(u[2 * pair + 1], u[2 * pair + 2])
        own_v[:, pair_lanes(pair)] = own_cells(v[2 * pair], v[2 * pair + 1])

    for stage in range(1, len(stages)):
        tops[stage] = gather_max(stage - 1)
        sent += len(stages[stage - 1])
        send_max(stage)
    top = gather_max(len(stages) - 1)
    for f in shared[2:]:
        v_copies[f].start()

    top = top[0:1, 0:1] + 6.0
    centre = (top + CUTOFF) / 2.0
    width = (top - CUTOFF) / 2.0
    away = centre - SHIFT
    alpha = 2.0 / (width * width)
    beta = -2.0 * away * alpha
    gamma = away * away * alpha - 1.0

    r = alpha * own_v[...] + beta * own_u[...] + gamma * own_w[...]
    r_s = split(r)
    gram = dot3(r_s, r_s, NT)
    rest_faces[...] = dot(pick[...], r_s[0], NT) + dot(pick[...], r_s[1], NT)
    sigma = jnp.sqrt(jnp.sum(jnp.sum(gram * gram, axis=1, keepdims=True), axis=0, keepdims=True))
    eye = flag(iota((rows, rows), 0) == iota((rows, rows), 1))
    product = gram * (1.0 / sigma)

    def newton(step, state):
        product, inverse = state
        factor = 1.5 * eye - 0.5 * product
        factor_s = split(factor)
        once = dot3(split(product), factor_s)
        inverse = dot3(split(inverse), factor_s)
        return dot3(split(once), factor_s), inverse

    product, inverse = lax.fori_loop(0, NEWTON - 1, newton, (product, eye))
    inverse = dot3(split(inverse), split(1.5 * eye - 0.5 * product))
    root = inverse * lax.rsqrt(sigma)
    root_s = split(root)

    rest_faces_s = split(rest_faces[...])
    facet[...] = dot3(rest_faces_s, root_s, NT)
    face_copies = []
    for f, offset in enumerate(faces):
        if sizes[f // 2] > 2:
            face_copies.append((f, pl.ds(f * area, area), pl.ds((f ^ 1) * area, area), offset))
        elif f % 2 == 0:
            both = pl.ds(f * area, 2 * area)
            face_copies.append((f, both, both, offset))
    for f, here, there, offset in face_copies:
        copy = remote(facet.at[here, :], ft_in.at[there, :], f_send, f_recv, offset)
        copy.start()

    facet_s = split(facet[...])
    inverse_width = 1.0 / width
    slots = []
    for f in range(6):
        slots.append(rest_faces[pl.ds((f if sizes[f // 2] > 2 else f ^ 1) * area, area), :])
    slots_s = split(jnp.concatenate(slots, axis=0))
    couple = split((-0.5 * inverse_width) * dot3(root_s, slots_s, NT))
    own_wide = dot2(wide[pl.ds(lower, length), :], select[0])
    own_odd = pltpu.roll(own_wide, area, 1)
    own_potential = jnp.concatenate(
        [own_wide[k : k + 1, :] + own_odd[k + 1 : k + 2, :] for k in range(0, length, 2)], axis=1
    )
    around = jnp.zeros_like(r)
    for stride in (area, length, 1):
        coordinate = lax.rem(lax.div(cell, stride), length)
        around = around + flag(coordinate > 0) * pltpu.roll(r, stride, 1)
        around = around + flag(coordinate < length - 1) * pltpu.roll(r, cells - stride, 1)
    boxed = (3.0 + own_potential) * r - 0.5 * around
    energy = dot3(split(boxed), r_s, NT)
    block = dot3(split(dot3(root_s, split(energy))), root_s, NT)
    diagonal = split(inverse_width * (block - centre * eye))

    prior = coef[...]
    current = dot3(diagonal, split(prior))
    finish(tiles.at[pl.ds(0, own)], tile_send)
    for stage in range(len(stages)):
        finish(tops_in.at[pl.ds(0, len(stages[stage]))], top_send.at[stage])
    finish(v_in.at[pl.ds(0, len(shared))], v_send)
    finish(v_in.at[pl.ds(0, len(shared))], v_recv)
    came = [split(v_in[shared.index(f ^ 1 if f ^ 1 in shared else f)]) for f in range(6)]
    carried = []
    finish(ft_in, f_recv)
    for f in range(6):
        carried.append(dot3(split(ft_in[pl.ds(f * area, area), :]), came[f]))
    current = current + dot3(couple, split(jnp.concatenate(carried, axis=0)))

    def send_projected(number, part, vectors):
        p_out[number, part] = dot3(facet_s, split(vectors))
        for f, here, there, offset in face_copies:
            copy = remote(
                p_out.at[number, part, here, :], p_in.at[number, part, there, :],
                p_send.at[number, part], p_recv.at[number, part], offset,
            )
            copy.start()

    prior = [prior[:, k * half : (k + 1) * half] for k in range(PARTS)]
    current = [current[:, k * half : (k + 1) * half] for k in range(PARTS)]
    for part in range(PARTS):
        send_projected(0, part, current[part])
    finish(facet, f_send)
    for number in range(2):
        following = []
        for part in range(PARTS):
            mine = 2.0 * dot3(diagonal, split(current[part])) - prior[part]
            if number == 1:
                finish(p_out.at[0, part], p_send.at[0, part])
            finish(p_in.at[number, part], p_recv.at[number, part])
            mine = mine + 2.0 * dot3(couple, split(p_in[number, part]))
            following.append(mine)
            if number == 0:
                send_projected(1, part, mine)
            else:
                out_ref[:, pl.ds(part * half, half)] = mine
        prior, current = current, following

    for part in range(PARTS):
        finish(p_out.at[1, part], p_send.at[1, part])


def per_device(sizes, orbitals, potential, coefficients):
    length = potential.shape[0]
    rows, cells = orbitals.shape[-2:]
    cols = coefficients.shape[-1]
    doubled, area = 2 * length, length * length
    plane, lanes = doubled * doubled, length * doubled
    stages = max_stages(sizes)
    top_copies = max(sum(len(stage) for stage in stages), 1)
    dma = pltpu.SemaphoreType.DMA
    result = pl.pallas_call(
        functools.partial(kernel, length, sizes),
        out_shape=jax.ShapeDtypeStruct((rows, cols), F32),
        in_specs=[pl.BlockSpec(memory_space=pltpu.HBM)] * 3,
        out_specs=pl.BlockSpec(memory_space=pltpu.VMEM),
        scratch_shapes=[
            pltpu.VMEM((plane, plane), BF16),
            pltpu.VMEM((2, plane, 2 * area), BF16),
            pltpu.VMEM((6 * area, length * area), BF16),
            pltpu.VMEM((rows, (length + 4) * plane), F32),
            pltpu.VMEM((length, length, length), F32),
            pltpu.VMEM((rows, cols), F32),
            pltpu.VMEM((8, length, lanes), F32),
            pltpu.VMEM((len(stages), 8, 128), F32),
            pltpu.VMEM((top_copies, 8, 128), F32),
            pltpu.VMEM((doubled, plane), F32),
            pltpu.VMEM((length + 2, rows, plane), F32),
            pltpu.VMEM((length, rows, plane), F32),
            pltpu.VMEM((rows, length * area), F32),
            pltpu.VMEM((rows, length * area), F32),
            pltpu.VMEM((rows, length * area), F32),
            pltpu.VMEM((6 * area, rows), F32),
            pltpu.VMEM((6 * area, rows), F32),
            pltpu.VMEM((6 * area, rows), F32),
            pltpu.VMEM((6, rows, cols), F32),
            pltpu.VMEM((2, PARTS, 6 * area, cols // PARTS), F32),
            pltpu.VMEM((2, PARTS, 6 * area, cols // PARTS), F32),
            dma((3,)),
            dma,
            dma,
            dma((max(len(stages), 1),)),
            dma((max(len(stages), 1),)),
            dma,
            dma,
            dma,
            dma,
            dma((2, PARTS)),
            dma((2, PARTS)),
        ],
        compiler_params=pltpu.CompilerParams(
            collective_id=0, has_side_effects=True, vmem_limit_bytes=60 * 1024 * 1024
        ),
    )(orbitals.reshape(rows, cells), potential, coefficients.reshape(rows, cols))
    return result.reshape(coefficients.shape)


def solution(mesh):
    sizes = tuple(mesh.shape[a] for a in AXES)
    placed = (P("gx", "gy", "gz", None, None), P("gx", "gy", "gz"), P("gx", "gy", "gz", None, None))
    return jax.shard_map(
        functools.partial(per_device, sizes),
        mesh=mesh,
        in_specs=placed,
        out_specs=P("gx", "gy", "gz", None, None),
        check_vma=False,
    )
```
